32 devices in a mesh: rows: 8 (over z, y), cols: 4 (over x, core).
Axes of the slice: x: 2, y: 2, z: 4, core: 2. Of those that a mesh axis runs over, the one named last changes fastest.
Arguments:
- series: float32 [300, 16384], P(None, ('rows', 'cols')), may hold values from -6 to 6
- point_order: int32 [16384], P('rows'), may hold values from 0 to 16383, as said below
- step_block: int32 [8], replicated, may hold values from 0 to 15, as said below
- panel: float32 [16384, 8192], P('rows', 'cols'), may hold values from -0.09375 to 0.09375
- diag_inverse: float32 [16384, 1024], P('rows'), may hold values from -0.09375 to 1.09375
Outputs:
- solved: float32 [8192, 300], P(('rows', 'cols'))
- residual: float32 [16384, 300], P(('rows', 'cols'))
The draws below stay inside these ranges and needn't reach their ends.
Inputs may be any that keep to these rules, and one draw needn't show every extreme that they name: Within each group of 2048 consecutive points, point_order is a permutation of the same group's indices. `step_block`: step k lies in block rows k * 2 + c to k * 2 + c + 1, with c = 0; the first step takes the first row of its range and the last step the last row of its range.
All inputs are finite; a program needn't handle non-finite values.
Results may differ from the reference program's by a relative error of at most 0.00014.
Values sent between devices are 32-bit elements; how exact they have to be, the bound alone decides.
No kernel may reach another device: no remote copies, remote signals or barrier semaphores. Data moves between devices by JAX's collectives and lax.ppermute only.
A program may use at most 128 MiB of HBM per device.

```python
import jax
import jax.numpy as jnp
from jax import lax

BS = 1024
DATES = 300
STEPS = 8
BR_DEV = 2
NBLK = 16
POINTS = 16384
SOLVED = 8192


def draw_point_order(key, part):
    group_size = BR_DEV * BS
    groups = POINTS // group_size
    keys = jax.random.split(key, groups)
    orders = jax.vmap(lambda single: jax.random.permutation(single, group_size))(keys)
    offsets = jnp.arange(groups, dtype=jnp.int32)[:, None] * group_size
    return (orders.astype(jnp.int32) + offsets).reshape(-1)


def draw_step_block(key, part):
    second = jax.random.fold_in(key, 11)
    groups = NBLK // BR_DEV
    offset = groups - STEPS
    slots = jax.random.randint(second, (STEPS,), 0, BR_DEV)
    positions = jnp.arange(STEPS, dtype=jnp.int32)
    slots = jnp.where(positions == 0, 0, slots)
    slots = jnp.where(positions == STEPS - 1, BR_DEV - 1, slots)
    owners = positions + offset
    return (owners * BR_DEV + slots).astype(jnp.int32)


def draw_diag_inverse(key, part):
    total_rows = NBLK * BS
    noise = jnp.clip(jax.random.normal(key, (total_rows, BS), jnp.float32), -6.0, 6.0)
    identity = (jnp.arange(total_rows)[:, None] % BS == jnp.arange(BS)[None, :]).astype(jnp.float32)
    return identity + 0.5 * noise * BS ** (-0.5)


def block_levels(key, dims, cuts, least, top_value):
    def one(position, blocks):
        draws = jax.random.uniform(jax.random.fold_in(jax.random.fold_in(key, 6), position), (blocks,), jnp.float32, least / len(cuts), top_value / len(cuts))
        return jnp.repeat(jnp.exp(draws), dims[position] // blocks).reshape((-1,) + (1,) * (len(dims) - position - 1))

    gain = one(*cuts[0])
    for cut in cuts[1:]:
        gain = gain * one(*cut)
    return gain


def bell_draw(own_key, extent, width, bound, cuts=(), kind=jnp.bfloat16):
    factor_of = block_levels(own_key, extent, cuts, -0.22, 0.18) if cuts else 1.0
    values = jax.random.normal(own_key, extent, jnp.float32) * width * factor_of
    return jnp.minimum(jnp.maximum(values, -bound), bound).astype(kind)


def setup_inputs(seed: int = 0) -> dict:
    arg_keys = jax.random.split(jax.random.key(seed), 6)
    return {
        "series": bell_draw(arg_keys[0], (DATES, POINTS), 1.0, 6.0, ((1, 32),), jnp.float32),
        "point_order": draw_point_order(jax.random.fold_in(arg_keys[5], 71), 0),
        "step_block": draw_step_block(jax.random.fold_in(arg_keys[5], 71), 0),
        "panel": bell_draw(arg_keys[3], (POINTS, SOLVED), (4 * STEPS * BS // 9) ** -0.5, 0.09375, ((0, 8), (1, 4)), jnp.float32),
        "diag_inverse": draw_diag_inverse(jax.random.fold_in(arg_keys[5], 71), 0),
    }


def reference(series, point_order, step_block, panel, diag_inverse):
    right_side = jnp.take(series, point_order, axis=1).T
    highest = lax.Precision.HIGHEST
    pieces = []
    for section in range(STEPS):
        start = (step_block[section] * BS).astype(jnp.int32)
        partial_value = jnp.zeros((BS, DATES), jnp.float32)
        for earlier in range(section):
            factor_block = lax.dynamic_slice(panel, (start, jnp.int32(earlier * BS)), (BS, BS))
            partial_value = partial_value + jnp.dot(factor_block, pieces[earlier], precision=highest, preferred_element_type=jnp.float32)
        pivot = lax.dynamic_slice(right_side, (start, jnp.int32(0)), (BS, DATES)) - partial_value
        inverse = lax.dynamic_slice(diag_inverse, (start, jnp.int32(0)), (BS, BS))
        pieces.append(jnp.dot(inverse, pivot, precision=highest, preferred_element_type=jnp.float32))
    solved = jnp.concatenate(pieces, axis=0)
    residual = right_side - jnp.dot(panel, solved, precision=highest, preferred_element_type=jnp.float32)
    return solved, residual
```

```python
import jax
import jax.numpy as jnp
from jax import lax
from jax.experimental import pallas as pl
from jax.experimental.pallas import tpu as pltpu
from jax.sharding import PartitionSpec as P

STEPS = 8
CHUNKS = 4
LINE_CHUNKS = 4
TILE = 512


def split_hi(value):
    return lax.reduce_precision(value, 8, 7)


def halves(value):
    high = value.astype(jnp.bfloat16)
    return high, (value - high.astype(jnp.float32)).astype(jnp.bfloat16)


def one_hot(index, depth):
    return (lax.broadcasted_iota(jnp.int32, (depth, index.shape[0]), 0) == index[None, :]).astype(jnp.bfloat16)


def picked(values, index):
    chosen = one_hot(index, values.shape[1])
    high = split_hi(values)
    low = split_hi(values - high)
    return (jnp.dot(high.astype(jnp.bfloat16), chosen, preferred_element_type=jnp.float32)
            + jnp.dot(low.astype(jnp.bfloat16), chosen, preferred_element_type=jnp.float32))


def dot_nt(left, right):
    return lax.dot_general(left, right, (((1,), (1,)), ((), ())), preferred_element_type=jnp.float32)


def in_vmem(value):
    return pltpu.with_memory_space_constraint(value, pltpu.VMEM)


def in_hbm(value):
    return pltpu.with_memory_space_constraint(value, pltpu.HBM)


def vmem_shape(shape, dtype):
    return pltpu.VMEM(shape, dtype)


def hbm_shape(shape, dtype):
    return pltpu.HBM(shape, dtype)


def factor_kernel(info, inverse_ref, panel_ref, *rest):
    high_ref, low_ref, inverse_high, inverse_low = rest[-4:]
    tile = pl.program_id(0)

    @pl.when(tile == 0)
    def _():
        high, low = halves(inverse_ref[...])
        inverse_high[...] = high
        inverse_low[...] = low

    @pl.when(tile <= info[1])
    def _():
        high, low = halves(panel_ref[...])
        value = (jnp.dot(inverse_high[...], high, preferred_element_type=jnp.float32)
                 + jnp.dot(inverse_low[...], high, preferred_element_type=jnp.float32)
                 + jnp.dot(inverse_high[...], low, preferred_element_type=jnp.float32))
        high, low = halves(value.T)
        high_ref[...] = high
        low_ref[...] = low


def chain_factors(info, diag_inverse, panel, tile, waited):
    block = diag_inverse.shape[1]
    depth = panel.shape[1]
    shape = vmem_shape((depth, block), jnp.bfloat16)
    return pl.pallas_call(
        factor_kernel,
        out_shape=[shape, shape],
        grid_spec=pltpu.PrefetchScalarGridSpec(
            num_scalar_prefetch=1,
            grid=(depth // tile,),
            in_specs=[
                pl.BlockSpec((block, block), lambda t, info: (info[0], 0)),
                pl.BlockSpec((block, tile), lambda t, info: (info[0], jnp.minimum(t, info[1]))),
            ] + [pl.BlockSpec(memory_space=pl.ANY)] * len(waited),
            out_specs=[pl.BlockSpec((tile, block), lambda t, info: (jnp.minimum(t, info[1]), 0))] * 2,
            scratch_shapes=[pltpu.VMEM((block, block), jnp.bfloat16)] * 2,
        ),
        compiler_params=pltpu.CompilerParams(vmem_limit_bytes=44 << 20),
        cost_estimate=pl.CostEstimate(
            flops=6 * block * block * depth, bytes_accessed=4 * block * (block + 2 * depth), transcendentals=0),
    )(info, in_hbm(diag_inverse), in_hbm(panel), *waited)


def start_kernel(info, *refs):
    shares, (place_ref, source_ref), (out_ref, inverse_ref, side, high, low, sem) = refs[:-8], refs[-8:-6], refs[-6:]
    dates, points = shares[0].shape
    lanes = high.shape[1]
    chunks, width, block = out_ref.shape
    tile = 256
    steps = block // tile

    @pl.when(info[1] == 1)
    def _():
        def inverse_rows(step):
            rows = pl.ds(pl.multiple_of(step * tile, tile), tile)
            source = pl.ds(pl.multiple_of(info[0] * block + step * tile, tile), tile)
            return pltpu.make_async_copy(source_ref.at[source], inverse_ref.at[rows], sem.at[step])

        for step in range(steps):
            inverse_rows(step).start()
        side[...] = jnp.zeros_like(side)
        for index, share in enumerate(shares):
            columns = pl.ds(index * points, points)
            first, second = halves(share[...])
            side[pl.ds(0, dates), columns] = first
            side[pl.ds(lanes, dates), columns] = second

        def order(step, carry):
            columns = pl.ds(pl.multiple_of(step * tile, tile), tile)
            places = lax.broadcasted_iota(jnp.int32, (side.shape[1], tile), 0)
            chosen = jnp.where(places == place_ref[:, columns], 1.0, 0.0).astype(jnp.bfloat16)
            both = jnp.dot(side[...], chosen, preferred_element_type=jnp.float32)
            first, second = halves((both[:lanes] + both[lanes:]).T)
            high[columns] = first
            low[columns] = second
            return carry

        def multiply(step, carry):
            rows = pl.ds(pl.multiple_of(step * tile, tile), tile)
            inverse_rows(step).wait()
            first, second = halves(inverse_ref[rows])
            value = (jnp.dot(first, high[...], preferred_element_type=jnp.float32)
                     + jnp.dot(second, high[...], preferred_element_type=jnp.float32)
                     + jnp.dot(first, low[...], preferred_element_type=jnp.float32)).T
            for chunk in range(chunks):
                out_ref[chunk, :, rows] = value[chunk * width:(chunk + 1) * width]
            return carry

        lax.fori_loop(0, steps, order, 0)
        lax.fori_loop(0, steps, multiply, 0)


def start_values(info, shares, place, diag_inverse, chunks, width, waited):
    block = diag_inverse.shape[1]
    dates, points = shares[0].shape
    lanes = -(-max(dates, chunks * width) // 128) * 128
    count = len(shares) + 2
    ordered = pltpu.VMEM((block, lanes), jnp.bfloat16)

    def kernel(info, *refs):
        start_kernel(info, *refs[:count], *refs[-6:])

    whole = pl.BlockSpec(memory_space=pltpu.VMEM)
    return pl.pallas_call(
        kernel,
        out_shape=vmem_shape((chunks, width, block), jnp.float32),
        in_specs=[pl.BlockSpec(memory_space=pltpu.SMEM)] + [whole] * (count - 1)
        + [pl.BlockSpec(memory_space=pl.ANY)] * (1 + len(waited)),
        out_specs=whole,
        scratch_shapes=[
            pltpu.VMEM((block, block), jnp.float32),
            pltpu.VMEM((2 * lanes, len(shares) * points), jnp.bfloat16),
            ordered,
            ordered,
            pltpu.SemaphoreType.DMA((block // 256,)),
        ],
        compiler_params=pltpu.CompilerParams(vmem_limit_bytes=28 << 20),
        cost_estimate=pl.CostEstimate(
            flops=10 * dates * block * block, bytes_accessed=4 * block * (block + 2 * dates), transcendentals=0),
    )(info, *map(in_vmem, shares), in_vmem(place), in_hbm(diag_inverse), *waited)


def slot_kernel(slot, chunks, sent, info, *refs):
    refs = list(refs)
    chain_ref = refs.pop(0) if sent[0] else None
    side_ref = refs.pop(0) if sent[1] else None
    up_ref = refs.pop(0) if sent[2] else None
    start_ref, start_rest_ref, high_ref, low_ref, out_ref, pair_ref, store_ref, sem = refs
    width, block = out_ref.shape
    first, second = pair_ref.at[pl.ds(0, width)], pair_ref.at[pl.ds(width, width)]
    chunk = slot - info[8]
    stored = (chunk >= 0) & (chunk < chunks)

    def keep_pair(action):
        @pl.when(stored & (info[1] == 2))
        def _():
            for stream in range(2):
                action(pltpu.make_async_copy(
                    pair_ref.at[pl.ds(stream * width, width)], store_ref.at[chunk, stream], sem.at[stream]))

    def keep_line(action):
        @pl.when(stored & (info[1] != 2))
        def _():
            action(pltpu.make_async_copy(out_ref, store_ref.at[chunk, info[9]], sem.at[0]))

    @pl.when(info[0] == 1)
    def _():
        out_ref[...] = side_ref[...] if sent[1] else jnp.zeros_like(out_ref)

    @pl.when(info[0] == 0)
    def _():
        out_ref[...] = jnp.zeros_like(out_ref)

    for code, ref in enumerate((side_ref, chain_ref, None if up_ref is None else up_ref.at[pl.ds(0, width)])):
        if ref is not None:
            @pl.when(info[1] == code)
            def _(ref=ref):
                first[...] = ref[...]
    for code, ref in enumerate((None if up_ref is None else up_ref.at[pl.ds(width, width)], chain_ref)):
        if ref is not None:
            @pl.when(info[2] == code)
            def _(ref=ref):
                second[...] = ref[...]

    keep_pair(lambda copy: copy.start())

    if any(sent):
        def step(tile, carry):
            per_stream = block // TILE
            rows = pl.ds(pl.multiple_of(tile // per_stream * width, 16), width)
            columns = pl.ds(pl.multiple_of(tile % per_stream * TILE, TILE), TILE)
            factor = pl.ds(pl.multiple_of(tile * TILE, TILE), TILE)
            high, low = halves(pair_ref[rows, columns])
            both = jnp.dot(jnp.concatenate([high, low], axis=0), high_ref[factor], preferred_element_type=jnp.float32)
            rest = jnp.dot(high, low_ref[factor], preferred_element_type=jnp.float32)
            out_ref[...] += (both[:width] + both[width:]) + rest
            return carry

        lax.fori_loop(0, info[3], step, 0)

    at = jnp.clip(slot - info[6], 0, chunks - 1)
    for code, ref in enumerate((start_ref, start_rest_ref)):
        @pl.when((info[4] == 1) & (info[10] == code))
        def _(ref=ref):
            out_ref[...] = ref[at] - out_ref[...]

    @pl.when(info[5] == 1)
    def _():
        second[...] = out_ref[...]

    if sent[1]:
        @pl.when(info[7] == 1)
        def _():
            out_ref[...] = side_ref[...]

    keep_line(lambda copy: copy.start())
    keep_line(lambda copy: copy.wait())
    keep_pair(lambda copy: copy.wait())


def advance(slot, info, received, start, start_rest, high, low, store, waited):
    chunks, width, block = start.shape
    sent = tuple(value is not None for value in received)
    operands = [in_vmem(value) for value in received if value is not None]
    operands += [in_vmem(start), in_vmem(start_rest), in_vmem(high), in_vmem(low)]
    count = len(operands)
    extra = list(waited) + ([] if store is None else [in_hbm(store)])

    def kernel(info, *refs):
        slot_kernel(slot, chunks, sent, info, *refs[:count], *refs[-4:])

    return pl.pallas_call(
        kernel,
        out_shape=[vmem_shape((width, block), jnp.float32), vmem_shape((2 * width, block), jnp.float32),
                   hbm_shape((chunks, 2, width, block), jnp.float32)],
        in_specs=[pl.BlockSpec(memory_space=pltpu.SMEM)] + [pl.BlockSpec(memory_space=pltpu.VMEM)] * count
        + [pl.BlockSpec(memory_space=pl.ANY)] * len(extra),
        out_specs=[pl.BlockSpec(memory_space=pltpu.VMEM)] * 2 + [pl.BlockSpec(memory_space=pl.ANY)],
        scratch_shapes=[pltpu.SemaphoreType.DMA((2,))],
        input_output_aliases={} if store is None else {count + len(extra): 2},
        compiler_params=pltpu.CompilerParams(vmem_limit_bytes=16 << 20),
        cost_estimate=pl.CostEstimate(
            flops=6 * width * block * high.shape[0], bytes_accessed=32 * width * block, transcendentals=0),
    )(info, *operands, *extra)


def fetch(chunk, info, store, arrays, waited):
    _, _, width, block = store.shape
    count = len(arrays)

    def kernel(info, store_ref, *refs):
        out_ref, sem = refs[-2:]

        def copies(action):
            @pl.when(info[0] == 0)
            def _():
                action(pltpu.make_async_copy(store_ref.at[chunk, info[1]], out_ref, sem))

        copies(lambda copy: copy.start())
        copies(lambda copy: copy.wait())
        for index in range(count):
            @pl.when(info[0] == index + 1)
            def _(index=index):
                out_ref[...] = refs[index][...]

    return pl.pallas_call(
        kernel,
        out_shape=vmem_shape((width, block), jnp.float32),
        in_specs=[pl.BlockSpec(memory_space=pltpu.SMEM), pl.BlockSpec(memory_space=pl.ANY)]
        + [pl.BlockSpec(memory_space=pltpu.VMEM)] * count + [pl.BlockSpec(memory_space=pl.ANY)] * len(waited),
        out_specs=pl.BlockSpec(memory_space=pltpu.VMEM),
        scratch_shapes=[pltpu.SemaphoreType.DMA],
        compiler_params=pltpu.CompilerParams(vmem_limit_bytes=16 << 20),
        cost_estimate=pl.CostEstimate(flops=0, bytes_accessed=0, transcendentals=0),
    )(info, in_hbm(store), *map(in_vmem, arrays), *waited)


def solved_shares(info, store, shares):
    chunks, _, width, block = store.shape
    size = block // shares

    def kernel(info, store_ref, *refs):
        outs, sem = refs[:-1], refs[-1]

        def copies(action):
            for chunk in range(chunks):
                for turn in range(shares):
                    columns = pl.ds(pl.multiple_of(info[1 + turn] * size, size), size)
                    action(pltpu.make_async_copy(store_ref.at[chunk, info[0], :, columns],
                                                 outs[turn].at[pl.ds(chunk * width, width)], sem.at[chunk, turn]))

        copies(lambda copy: copy.start())
        copies(lambda copy: copy.wait())

    return pl.pallas_call(
        kernel,
        out_shape=[vmem_shape((chunks * width, size), jnp.float32)] * shares,
        in_specs=[pl.BlockSpec(memory_space=pltpu.SMEM), pl.BlockSpec(memory_space=pl.ANY)],
        out_specs=[pl.BlockSpec(memory_space=pltpu.VMEM)] * shares,
        scratch_shapes=[pltpu.SemaphoreType.DMA((chunks, shares))],
        compiler_params=pltpu.CompilerParams(vmem_limit_bytes=16 << 20),
        cost_estimate=pl.CostEstimate(flops=0, bytes_accessed=0, transcendentals=0),
    )(info, in_hbm(store))


def turn_kernel(info, chunks, width, store_ref, *refs):
    lines, crossed, series_ref = refs[:chunks], refs[chunks:2 * chunks], refs[2 * chunks]
    high, low, side_high, side_low, raw, side, sem = refs[-7:]
    block = raw.shape[2]
    dates = series_ref.shape[0]
    total = chunks * width

    def copies(action):
        for chunk in range(chunks):
            rows = pl.ds(chunk * width, width)

            @pl.when(info[0] == 1)
            def _(chunk=chunk, rows=rows):
                for stream in range(2):
                    action(pltpu.make_async_copy(
                        store_ref.at[chunk, stream], raw.at[stream, rows], sem.at[2 * chunk + stream]))

            @pl.when(info[0] == 0)
            def _(chunk=chunk, rows=rows):
                action(pltpu.make_async_copy(lines[chunk], raw.at[info[1], rows], sem.at[2 * chunk]))
                action(pltpu.make_async_copy(crossed[chunk], raw.at[1 - info[1], rows], sem.at[2 * chunk + 1]))

    copies(lambda copy: copy.start())
    lanes = side.shape[0]
    side[...] = jnp.zeros_like(side)
    side[pl.ds(0, dates)] = series_ref[...]
    first, second = halves(side[...].T)
    side_high[...] = first
    side_low[...] = second
    raw[:, pl.ds(total, lanes - total)] = jnp.zeros((2, lanes - total, block), jnp.float32)
    copies(lambda copy: copy.wait())
    for stream in range(2):
        first, second = halves(raw[stream].T)
        high[pl.ds(stream * block, block)] = first
        low[pl.ds(stream * block, block)] = second


def turned(info, store, sources, series, waited):
    chunks, _, width, block = store.shape
    dates, points = series.shape
    lanes = -(-max(dates, chunks * width) // 128) * 128
    count = 2 + len(sources)

    def kernel(info, *refs):
        turn_kernel(info, chunks, width, *refs[:count], *refs[count + len(waited):])

    whole = pl.BlockSpec(memory_space=pltpu.VMEM)
    solved = vmem_shape((2 * block, lanes), jnp.bfloat16)
    side = vmem_shape((points, lanes), jnp.bfloat16)
    return pl.pallas_call(
        kernel,
        out_shape=[solved, solved, side, side],
        in_specs=[pl.BlockSpec(memory_space=pltpu.SMEM)] + [pl.BlockSpec(memory_space=pl.ANY)] * (1 + len(sources))
        + [whole] + [pl.BlockSpec(memory_space=pl.ANY)] * len(waited),
        out_specs=[whole] * 4,
        scratch_shapes=[
            pltpu.VMEM((2, lanes, block), jnp.float32),
            pltpu.VMEM((lanes, points), jnp.float32),
            pltpu.SemaphoreType.DMA((2 * chunks,)),
        ],
        compiler_params=pltpu.CompilerParams(vmem_limit_bytes=16 << 20),
        cost_estimate=pl.CostEstimate(flops=0, bytes_accessed=0, transcendentals=0),
    )(info, in_hbm(store), *sources, in_vmem(series), *waited)


def residual_kernel(info, first_tile, tiles, high, low, side_high, side_low, place_ref, panel_ref, *rest):
    out_ref, held, sem = rest[-3:]
    steps, rows = held.shape[:2]
    total = out_ref.shape[0]
    per_tile = steps // tiles

    def source_rows(step):
        start = info[2 + first_tile + step // per_tile] * (per_tile * rows) + step % per_tile * rows
        return pl.ds(pl.multiple_of(start, rows), rows)

    def panel_rows(step):
        return pltpu.make_async_copy(panel_ref.at[source_rows(step)], held.at[step], sem.at[step])

    for step in range(steps):
        panel_rows(step).start()

    def multiply(step, carry):
        panel_rows(step).wait()
        factor_high, factor_low = halves(held[step])
        product = (jnp.dot(factor_high, high[...], preferred_element_type=jnp.float32)
                   + jnp.dot(factor_high, low[...], preferred_element_type=jnp.float32)
                   + jnp.dot(factor_low, high[...], preferred_element_type=jnp.float32))
        places = lax.broadcasted_iota(jnp.int32, (rows, side_high.shape[0]), 1)
        chosen = jnp.where(places == place_ref[source_rows(step)], 1.0, 0.0).astype(jnp.bfloat16)
        value = (jnp.dot(chosen, side_high[...], preferred_element_type=jnp.float32)
                 + jnp.dot(chosen, side_low[...], preferred_element_type=jnp.float32)) - product
        out_ref[:, pl.ds(pl.multiple_of(step * rows, rows), rows)] = value.T[:total]
        return carry

    lax.fori_loop(0, steps, multiply, 0)


def residual_tiles(info, first_tile, tiles, size, total, parts, place, panel, waited):
    depth = panel.shape[1]
    rows = 256
    steps = tiles * size // rows

    def kernel(info, *refs):
        residual_kernel(info, first_tile, tiles, *refs[:6], *refs[-3:])

    whole = pl.BlockSpec(memory_space=pltpu.VMEM)
    return pl.pallas_call(
        kernel,
        out_shape=vmem_shape((total, tiles * size), jnp.float32),
        in_specs=[pl.BlockSpec(memory_space=pltpu.SMEM)] + [whole] * 5
        + [pl.BlockSpec(memory_space=pl.ANY)] * (1 + len(waited)),
        out_specs=whole,
        scratch_shapes=[pltpu.VMEM((steps, rows, depth), jnp.float32), pltpu.SemaphoreType.DMA((steps,))],
        compiler_params=pltpu.CompilerParams(vmem_limit_bytes=36 << 20),
        cost_estimate=pl.CostEstimate(
            flops=6 * total * tiles * size * depth, bytes_accessed=4 * tiles * size * depth, transcendentals=0),
    )(info, *map(in_vmem, parts), in_vmem(place), in_hbm(panel), *waited)


def add_kernel(left_ref, right_ref, out_ref):
    out_ref[...] = left_ref[...] + right_ref[:, pl.ds(0, out_ref.shape[1])]


def added(left, right):
    whole = pl.BlockSpec(memory_space=pltpu.VMEM)
    return pl.pallas_call(
        add_kernel,
        out_shape=vmem_shape(left.shape, left.dtype),
        in_specs=[whole] * 2,
        out_specs=whole,
        compiler_params=pltpu.CompilerParams(vmem_limit_bytes=16 << 20),
    )(in_vmem(left), in_vmem(right))


def make_line_body(row_count, col_count):
    levels = row_count // 2
    chunks = LINE_CHUNKS

    def flat(level, side, col):
        return (2 * level + side) * col_count + col

    def body(series, point_order, step_block, panel, diag_inverse):
        f32 = jnp.float32
        dates, own_points = series.shape
        block = diag_inverse.shape[1]
        group_rows, depth = panel.shape
        local_blocks = group_rows // block
        width = -(-dates // (16 * chunks)) * 16
        padded = width * chunks
        row = lax.axis_index("rows")
        col = lax.axis_index("cols")
        level, side = row // 2, row % 2

        def send(value, pairs):
            return lax.ppermute(value, ("rows", "cols"), pairs)

        def solver(step):
            return flat(step // 2, step % 2, max(step - 1, 0) // 2)

        def busy(start, slot):
            return 0 <= slot - start < chunks

        above, same = level > col, level == col
        second_solver = same & (side == 1)
        last = (side == 0) & (level == col + 1)
        origin = (row == 0) & (col == 0)
        is_solver = second_solver | last | origin

        shares = [series]
        for turn in range(1, col_count):
            pairs = []
            for step in range(STEPS):
                here = max(step - 1, 0) // 2
                pairs.append((flat(step // 2, step % 2, (here + turn) % col_count), flat(step // 2, step % 2, here)))
            shares.append(send(series, pairs))

        per_tile = 256
        top = levels - 1
        last_factor = jnp.where(above, depth // per_tile - 1, jnp.where(second_solver, block // per_tile - 1, 0))
        slot_index = step_block[row] % local_blocks
        local_order = point_order % group_rows
        block_order = lax.dynamic_slice(local_order, (slot_index * block,), (block,))
        place = (block_order // own_points - col) % col_count * own_points + block_order % own_points
        first_direct = 2 * top + 2
        arrived = jnp.where(origin, 0, jnp.where((col == top) & (level == top - 1), first_direct, 3 * col - level + 1))
        from_direct = (col == top) & (level < top - 1)
        stored_at = jnp.where(above, level + col + 1, jnp.where(from_direct, first_direct + 4 * chunks, arrived))
        own_place = jnp.where(local_order // own_points != col, -1, local_order % own_points)[:, None]
        def pack(*values):
            return jnp.stack([jnp.asarray(value).astype(jnp.int32) for value in values])

        factor_info = pack(slot_index, last_factor)
        start_info = pack(slot_index, origin)
        rest_info = pack(slot_index, is_solver & jnp.logical_not(origin))
        slot_info = pack(
            (above | second_solver) & (col > 0),
            jnp.where(above, 2, jnp.where(second_solver, 1, 0)),
            last,
            jnp.where(above, depth // TILE, jnp.where(second_solver, block // TILE, 0)),
            is_solver,
            second_solver,
            jnp.where(origin, 0, level + col + 1),
            jnp.logical_not(above | second_solver | origin),
            stored_at,
            side,
            jnp.logical_not(origin),
        )
        fetch_info = pack(jnp.where(from_direct, level + 1, 0), side)
        late_info = pack(jnp.where((col == top) & (level == top - 1), top, jnp.where(from_direct, level + 1, 0)), side)
        solved_info = pack(side, *[(col + turn) % col_count for turn in range(col_count)])
        residual_info = pack(above, side, col ^ 3, col ^ 1, col ^ 2, col)
        place = place[None, :]
        waited = [place, start_info, rest_info, slot_info, fetch_info, late_info, solved_info, residual_info, own_place]

        high, low = chain_factors(factor_info, diag_inverse, panel, per_tile, waited)
        start = start_values(start_info, shares, place, diag_inverse, chunks, width, [])

        chain_pairs = [(solver(step), solver(step + 1)) for step in range(STEPS - 1)]
        side_pairs = [(0, 0)]
        down_pairs, cross_pairs = [], []
        for c in range(col_count):
            for z in range(levels):
                for y in range(2):
                    if z > c:
                        side_pairs.append((flat(z, y, c), flat(z, y, c + 1)))
                        continue
                    cross_pairs.append((flat(z, y, c), flat(z, 1 - y, c)))
                    if z and (c < levels - 1 or z == c):
                        down_pairs.append((flat(z, y, c), flat(z - 1, y, c)))
        direct_pairs = [[(flat(top, y, top), flat(z, y, top)) for y in range(2)] for z in range(top)]
        late_pairs = direct_pairs[top - 1]
        mine, crossed, direct = [], [], []

        def send_direct():
            direct.append([send(out, direct_pairs[z]) for z in range(top - 1)])

        def cross(info, arrays, waited):
            mine.append(fetch(len(mine), info, store, arrays, mine[-1:] + waited))
            crossed.append(send(mine[-1], cross_pairs))

        out = pair = store = None
        start_rest = start
        last_solve = STEPS - 1 + chunks - 1
        for slot in range(last_solve + 1):
            received = [None, None, None]
            if slot:
                ups = [(flat(z, y, c), flat(z + 1, y, c)) for c in range(col_count) for z in range(c, levels - 1)
                       for y in range(2) if busy(z + c + 1, slot - 1)]
                received = [send(out, chain_pairs), send(out, side_pairs + down_pairs),
                            send(pair, ups) if ups else None]
            if slot >= first_direct:
                send_direct()
            out, pair, store = advance(slot, slot_info, received, start, start_rest, high, low, store,
                                       mine[-1:] + crossed[:-1][-1:])
            if slot == 0:
                start_rest = start_values(rest_info, shares, place, diag_inverse, chunks, width, [out])
            if slot >= first_direct:
                cross(fetch_info, direct[-1], [])

        send_direct()
        late = send(out, late_pairs)
        pieces = solved_shares(solved_info, store, col_count)
        delivered = []
        for turn in range(1, col_count):
            pairs = [(flat(z, y, z), flat(z, y, (z + turn) % col_count)) for z in range(levels) for y in range(2)]
            delivered.append(send(pieces[turn], pairs))
        cross(late_info, direct[-1] + [late], [pieces[0]])
        near = [(at * col_count + here, at * col_count + (here ^ 1))
                for at in range(row_count) for here in range(col_count)]
        far = [(at * col_count + here, at * col_count + (here ^ 2))
               for at in range(row_count) for here in range(col_count)]

        size = group_rows // col_count
        parts = turned(residual_info, store, mine + crossed, series, delivered)
        give = residual_tiles(residual_info, 0, 2, size, padded, parts, own_place, panel, [])
        moved = send(give, near)
        passed = residual_tiles(residual_info, 2, 1, size, padded, parts, own_place, panel, [give])
        passed = added(passed, moved)
        moved_far = send(passed, far)
        own = residual_tiles(residual_info, 3, 1, size, padded, parts, own_place, panel, [passed])
        solved = pieces[0]
        for turn in range(1, col_count):
            solved = jnp.where((col - level) % col_count == turn, delivered[turn - 1], solved)

        residual = ((own + moved[:, size:]) + moved_far)[:dates]
        return solved[:dates].T, residual.T

    return body


def make_body(row_count, col_count):
    base = row_count - STEPS

    def body(series, point_order, step_block, panel, diag_inverse):
        f32 = jnp.float32
        dates, own_points = series.shape
        block = diag_inverse.shape[1]
        group_rows = panel.shape[0]
        local_blocks = group_rows // block
        per = panel.shape[1] // block
        width = -(-dates // (8 * CHUNKS)) * 8
        padded = width * CHUNKS

        def column(step):
            return step // per

        solver_col = [0] + [column(step - 1) for step in range(1, STEPS)]

        def arrival(start, distance):
            if distance >= 1:
                return start + -(-distance // 2)
            return start + 1 + (-distance) // 2

        def fits(hop):
            for step in range(STEPS):
                for earlier in range(step):
                    due = hop * step - (solver_col[step] - column(earlier))
                    if arrival(hop * earlier, step - earlier) > due:
                        return False
            return True

        hop = 1
        while not fits(hop):
            hop += 1

        def flat(row, col):
            return row * col_count + col

        def busy(start, slot):
            return 0 <= slot - start < CHUNKS

        row = lax.axis_index("rows")
        col = lax.axis_index("cols")
        step_here = row - base
        has_step = step_here >= 0
        step_safe = jnp.maximum(step_here, 0)
        solver_here = jnp.where(step_safe == 0, 0, (step_safe - 1) // per)
        is_solver = has_step & (col == solver_here)

        def send(value, pairs):
            return lax.ppermute(value, ("rows", "cols"), pairs)

        first_row = step_block[step_safe] % local_blocks * block
        inverse = lax.dynamic_slice(diag_inverse, (first_row, jnp.int32(0)), (block, block))
        factor = lax.dynamic_slice(panel, (first_row, jnp.int32(0)), (block, per * block))
        chain_factor = lax.dot_general(
            factor, inverse, (((0,), (1,)), ((), ())),
            precision=lax.Precision.HIGH, preferred_element_type=f32)

        shares = [series]
        for turn in range(1, col_count):
            pairs = [
                (flat(base + step, (solver_col[step] + turn) % col_count), flat(base + step, solver_col[step]))
                for step in range(STEPS)
            ]
            shares.append(send(series, pairs))
        gathered = jnp.concatenate(shares, axis=1)
        local_order = point_order % group_rows

        block_order = lax.dynamic_slice(local_order, (first_row,), (block,))
        place = (block_order // own_points - col) % col_count * own_points + block_order % own_points
        side = picked(gathered, place)
        start_value = lax.dot_general(
            side, inverse, (((1,), (1,)), ((), ())),
            precision=lax.Precision.HIGH, preferred_element_type=f32)
        start_value = jnp.pad(start_value, ((0, padded - dates), (0, 0))).reshape(CHUNKS, width, block)

        zero = jnp.zeros((width, block), f32)
        held = [jnp.zeros((CHUNKS + 1, width, block), f32) for _ in range(per)]
        latest = [zero] * per
        outgoing = None
        streams = [col * per + index for index in range(per)]
        gaps = [step_here - stream for stream in streams]
        starts = [hop * stream for stream in streams]

        def arrival_here(start, gap):
            return jnp.where(gap >= 1, start + (gap + 1) // 2, start + 1 + (-gap) // 2)

        arrivals = [arrival_here(start, gap) for start, gap in zip(starts, gaps)]
        due = hop * step_here - (solver_here - col)

        def pick_chunk(values, chunk):
            return lax.dynamic_index_in_dim(values, jnp.clip(chunk, 0, CHUNKS - 1), 0, keepdims=False)

        last_slot = max(arrival(hop * step, place_row - base - step)
                        for step in range(STEPS) for place_row in range(row_count)) + CHUNKS - 1
        for slot in range(last_slot + 1):
            before = slot - 1
            one_up, two_up, level, one_down, added = [], [], [], [], []
            if before >= 0:
                for step in range(STEPS):
                    source = flat(base + step, solver_col[step])
                    if busy(hop * step, before):
                        if step + 1 < STEPS:
                            one_up.append((source, flat(base + step + 1, column(step))))
                        if step + 2 < STEPS:
                            two_up.append((source, flat(base + step + 2, column(step))))
                        if solver_col[step] != column(step):
                            level.append((source, flat(base + step, column(step))))
                        if base + step >= 1:
                            one_down.append((source, flat(base + step - 1, column(step))))
                    for from_col in range(solver_col[step]):
                        if busy(hop * step - (solver_col[step] - from_col), before):
                            added.append((flat(base + step, from_col), flat(base + step, from_col + 1)))
            from_one_up = send(outgoing, one_up) if one_up else zero
            incoming = send(outgoing, added) if added else zero
            from_two_up = send(outgoing, two_up) if two_up else zero
            from_level = send(outgoing, level) if level else zero
            from_one_down = send(outgoing, one_down) if one_down else zero
            received_up, received_down = [], []
            for index in range(per):
                upward, downward = [], []
                for stream in range(index, STEPS, per):
                    for at in range(row_count):
                        gap = at - base - stream
                        if busy(arrival(hop * stream, gap), before):
                            if gap >= 1 and at + 2 < row_count:
                                upward.append((flat(at, column(stream)), flat(at + 2, column(stream))))
                            if gap <= 0 and at >= 2:
                                downward.append((flat(at, column(stream)), flat(at - 2, column(stream))))
                received_up.append(send(latest[index], upward) if upward else zero)
                received_down.append(send(latest[index], downward) if downward else zero)

            inputs = []
            for index in range(per):
                gap = gaps[index]
                up = jnp.where(gap == 1, from_one_up, jnp.where(gap == 2, from_two_up, received_up[index]))
                same = jnp.where(col == solver_here, zero if outgoing is None else outgoing, from_level)
                down = jnp.where(gap == 0, same, jnp.where(gap == -1, from_one_down, received_down[index]))
                got = jnp.where(gap >= 1, up, down)
                chunk = slot - arrivals[index]
                valid = (chunk >= 0) & (chunk < CHUNKS)
                needed = slot - due
                ready = jnp.where(needed == chunk, up, pick_chunk(held[index], needed))
                inputs.append(jnp.where((gap >= 1) & has_step, ready, 0))
                held[index] = lax.dynamic_update_index_in_dim(
                    held[index], got, jnp.where(valid, chunk, CHUNKS), 0)
                latest[index] = got
            if slot <= hop * (STEPS - 1) + CHUNKS - 1:
                total = incoming + jnp.dot(
                    jnp.concatenate(inputs, axis=1), chain_factor,
                    precision=lax.Precision.HIGH, preferred_element_type=f32)
                outgoing = jnp.where(is_solver, pick_chunk(start_value, slot - due) - total, total)

        whole = [values[:CHUNKS].reshape(padded, block)[:dates] for values in held]
        out_rows = STEPS * block // (row_count * col_count)

        def wanted(at):
            return at * col_count * out_rows // block

        source_col = row * col_count * out_rows // block // per
        stream_index = row * col_count * out_rows // block % per
        chosen = whole[0]
        for index in range(1, per):
            chosen = jnp.where(stream_index == index, whole[index], chosen)

        def piece(target):
            first = (row * col_count + target) * out_rows % block
            return lax.dynamic_slice(chosen, (jnp.int32(0), first), (dates, out_rows))

        solved = piece(col)
        for turn in range(1, col_count):
            pairs = [
                (flat(at, column(wanted(at))), flat(at, (column(wanted(at)) + turn) % col_count))
                for at in range(row_count)
            ]
            moved = send(piece((col + turn) % col_count), pairs)
            solved = jnp.where((col - source_col) % col_count == turn, moved, solved)

        away = local_order // own_points != col
        own_place = jnp.where(away, -1, local_order % own_points)
        product = lax.dot_general(
            jnp.concatenate(whole, axis=1), panel, (((1,), (1,)), ((), ())),
            precision=lax.Precision.HIGH, preferred_element_type=f32)
        left = picked(series, own_place) - product
        distance = 1
        parts = left.reshape(dates, col_count, group_rows // col_count)
        pieces = [parts[:, index] for index in range(col_count)]
        while distance < col_count:
            bit = (col // distance) % 2
            keep, give = [], []
            for index in range(0, len(pieces), 2):
                keep.append(jnp.where(bit == 0, pieces[index], pieces[index + 1]))
                give.append(jnp.where(bit == 0, pieces[index + 1], pieces[index]))
            pairs = [(flat(at, here), flat(at, here ^ distance)) for at in range(row_count) for here in range(col_count)]
            moved = send(jnp.concatenate(give, axis=1) if len(give) > 1 else give[0], pairs)
            size = group_rows // col_count
            pieces = [value + moved[:, index * size:(index + 1) * size] for index, value in enumerate(keep)]
            distance *= 2
        return solved.T, pieces[0].T

    return body


def solution(mesh):
    in_specs = (P(None, ("rows", "cols")), P("rows"), P(), P("rows", "cols"), P("rows", None))
    out_specs = (P(("rows", "cols"), None), P(("rows", "cols"), None))
    row_count, col_count = mesh.shape["rows"], mesh.shape["cols"]
    lines = row_count == STEPS and 2 * col_count == STEPS
    body = (make_line_body if lines else make_body)(row_count, col_count)
    return jax.shard_map(body, mesh=mesh, in_specs=in_specs, out_specs=out_specs, check_vma=False)
```

```python
import jax
import jax.numpy as jnp
from jax import lax
from jax.experimental import pallas as pl
from jax.experimental.pallas import tpu as pltpu
from jax.sharding import PartitionSpec as P

STEPS = 8
CHUNKS = 4
LINE_CHUNKS = 4
TILE = 512


def split_hi(value):
    return lax.reduce_precision(value, 8, 7)


def halves(value):
    high = value.astype(jnp.bfloat16)
    return high, (value - high.astype(jnp.float32)).astype(jnp.bfloat16)


def one_hot(index, depth):
    return (lax.broadcasted_iota(jnp.int32, (depth, index.shape[0]), 0) == index[None, :]).astype(jnp.bfloat16)


def picked(values, index):
    chosen = one_hot(index, values.shape[1])
    high = split_hi(values)
    low = split_hi(values - high)
    return (jnp.dot(high.astype(jnp.bfloat16), chosen, preferred_element_type=jnp.float32)
            + jnp.dot(low.astype(jnp.bfloat16), chosen, preferred_element_type=jnp.float32))


def dot_nt(left, right):
    return lax.dot_general(left, right, (((1,), (1,)), ((), ())), preferred_element_type=jnp.float32)


def in_vmem(value):
    return pltpu.with_memory_space_constraint(value, pltpu.VMEM)


def in_hbm(value):
    return pltpu.with_memory_space_constraint(value, pltpu.HBM)


def vmem_shape(shape, dtype):
    return pltpu.VMEM(shape, dtype)


def hbm_shape(shape, dtype):
    return pltpu.HBM(shape, dtype)


def factor_kernel(info, inverse_ref, panel_ref, *rest):
    high_ref, low_ref, inverse_high, inverse_low = rest[-4:]
    tile = pl.program_id(0)

    @pl.when(tile == 0)
    def _():
        high, low = halves(inverse_ref[...])
        inverse_high[...] = high
        inverse_low[...] = low

    @pl.when(tile <= info[1])
    def _():
        high, low = halves(panel_ref[...])
        value = (jnp.dot(inverse_high[...], high, preferred_element_type=jnp.float32)
                 + jnp.dot(inverse_low[...], high, preferred_element_type=jnp.float32)
                 + jnp.dot(inverse_high[...], low, preferred_element_type=jnp.float32))
        high, low = halves(value.T)
        high_ref[...] = high
        low_ref[...] = low


def chain_factors(info, diag_inverse, panel, tile, waited):
    block = diag_inverse.shape[1]
    depth = panel.shape[1]
    shape = vmem_shape((depth, block), jnp.bfloat16)
    return pl.pallas_call(
        factor_kernel,
        out_shape=[shape, shape],
        grid_spec=pltpu.PrefetchScalarGridSpec(
            num_scalar_prefetch=1,
            grid=(depth // tile,),
            in_specs=[
                pl.BlockSpec((block, block), lambda t, info: (info[0], 0)),
                pl.BlockSpec((block, tile), lambda t, info: (info[0], jnp.minimum(t, info[1]))),
            ] + [pl.BlockSpec(memory_space=pl.ANY)] * len(waited),
            out_specs=[pl.BlockSpec((tile, block), lambda t, info: (jnp.minimum(t, info[1]), 0))] * 2,
            scratch_shapes=[pltpu.VMEM((block, block), jnp.bfloat16)] * 2,
        ),
        compiler_params=pltpu.CompilerParams(vmem_limit_bytes=44 << 20),
        cost_estimate=pl.CostEstimate(
            flops=6 * block * block * depth, bytes_accessed=4 * block * (block + 2 * depth), transcendentals=0),
    )(info, in_hbm(diag_inverse), in_hbm(panel), *waited)


def start_kernel(info, *refs):
    shares, (place_ref, source_ref), (out_ref, inverse_ref, side, high, low, sem) = refs[:-8], refs[-8:-6], refs[-6:]
    dates, points = shares[0].shape
    lanes = high.shape[1]
    chunks, width, block = out_ref.shape
    tile = 256
    steps = block // tile

    @pl.when(info[1] == 1)
    def _():
        def inverse_rows(step):
            rows = pl.ds(pl.multiple_of(step * tile, tile), tile)
            source = pl.ds(pl.multiple_of(info[0] * block + step * tile, tile), tile)
            return pltpu.make_async_copy(source_ref.at[source], inverse_ref.at[rows], sem.at[step])

        for step in range(steps):
            inverse_rows(step).start()
        side[...] = jnp.zeros_like(side)
        for index, share in enumerate(shares):
            columns = pl.ds(index * points, points)
            first, second = halves(share[...])
            side[pl.ds(0, dates), columns] = first
            side[pl.ds(lanes, dates), columns] = second

        def order(step, carry):
            columns = pl.ds(pl.multiple_of(step * tile, tile), tile)
            places = lax.broadcasted_iota(jnp.int32, (side.shape[1], tile), 0)
            chosen = jnp.where(places == place_ref[:, columns], 1.0, 0.0).astype(jnp.bfloat16)
            both = jnp.dot(side[...], chosen, preferred_element_type=jnp.float32)
            first, second = halves((both[:lanes] + both[lanes:]).T)
            high[columns] = first
            low[columns] = second
            return carry

        def multiply(step, carry):
            rows = pl.ds(pl.multiple_of(step * tile, tile), tile)
            inverse_rows(step).wait()
            first, second = halves(inverse_ref[rows])
            value = (jnp.dot(first, high[...], preferred_element_type=jnp.float32)
                     + jnp.dot(second, high[...], preferred_element_type=jnp.float32)
                     + jnp.dot(first, low[...], preferred_element_type=jnp.float32)).T
            for chunk in range(chunks):
                out_ref[chunk, :, rows] = value[chunk * width:(chunk + 1) * width]
            return carry

        lax.fori_loop(0, steps, order, 0)
        lax.fori_loop(0, steps, multiply, 0)


def start_values(info, shares, place, diag_inverse, chunks, width, waited):
    block = diag_inverse.shape[1]
    dates, points = shares[0].shape
    lanes = -(-max(dates, chunks * width) // 128) * 128
    count = len(shares) + 2
    ordered = pltpu.VMEM((block, lanes), jnp.bfloat16)

    def kernel(info, *refs):
        start_kernel(info, *refs[:count], *refs[-6:])

    whole = pl.BlockSpec(memory_space=pltpu.VMEM)
    return pl.pallas_call(
        kernel,
        out_shape=vmem_shape((chunks, width, block), jnp.float32),
        in_specs=[pl.BlockSpec(memory_space=pltpu.SMEM)] + [whole] * (count - 1)
        + [pl.BlockSpec(memory_space=pl.ANY)] * (1 + len(waited)),
        out_specs=whole,
        scratch_shapes=[
            pltpu.VMEM((block, block), jnp.float32),
            pltpu.VMEM((2 * lanes, len(shares) * points), jnp.bfloat16),
            ordered,
            ordered,
            pltpu.SemaphoreType.DMA((block // 256,)),
        ],
        compiler_params=pltpu.CompilerParams(vmem_limit_bytes=28 << 20),
        cost_estimate=pl.CostEstimate(
            flops=10 * dates * block * block, bytes_accessed=4 * block * (block + 2 * dates), transcendentals=0),
    )(info, *map(in_vmem, shares), in_vmem(place), in_hbm(diag_inverse), *waited)


def slot_kernel(slot, chunks, sent, info, *refs):
    refs = list(refs)
    chain_ref = refs.pop(0) if sent[0] else None
    side_ref = refs.pop(0) if sent[1] else None
    up_ref = refs.pop(0) if sent[2] else None
    start_ref, start_rest_ref, high_ref, low_ref, out_ref, pair_ref, store_ref, sem = refs
    width, block = out_ref.shape
    first, second = pair_ref.at[pl.ds(0, width)], pair_ref.at[pl.ds(width, width)]
    chunk = slot - info[8]
    stored = (chunk >= 0) & (chunk < chunks)

    def keep_pair(action):
        @pl.when(stored & (info[1] == 2))
        def _():
            for stream in range(2):
                action(pltpu.make_async_copy(
                    pair_ref.at[pl.ds(stream * width, width)], store_ref.at[chunk, stream], sem.at[stream]))

    def keep_line(action):
        @pl.when(stored & (info[1] != 2))
        def _():
            action(pltpu.make_async_copy(out_ref, store_ref.at[chunk, info[9]], sem.at[0]))

    @pl.when(info[0] == 1)
    def _():
        out_ref[...] = side_ref[...] if sent[1] else jnp.zeros_like(out_ref)

    @pl.when(info[0] == 0)
    def _():
        out_ref[...] = jnp.zeros_like(out_ref)

    for code, ref in enumerate((side_ref, chain_ref, None if up_ref is None else up_ref.at[pl.ds(0, width)])):
        if ref is not None:
            @pl.when(info[1] == code)
            def _(ref=ref):
                first[...] = ref[...]
    for code, ref in enumerate((None if up_ref is None else up_ref.at[pl.ds(width, width)], chain_ref)):
        if ref is not None:
            @pl.when(info[2] == code)
            def _(ref=ref):
                second[...] = ref[...]

    keep_pair(lambda copy: copy.start())

    if any(sent):
        def step(tile, carry):
            per_stream = block // TILE
            rows = pl.ds(pl.multiple_of(tile // per_stream * width, 16), width)
            columns = pl.ds(pl.multiple_of(tile % per_stream * TILE, TILE), TILE)
            factor = pl.ds(pl.multiple_of(tile * TILE, TILE), TILE)
            high, low = halves(pair_ref[rows, columns])
            both = jnp.dot(jnp.concatenate([high, low], axis=0), high_ref[factor], preferred_element_type=jnp.float32)
            rest = jnp.dot(high, low_ref[factor], preferred_element_type=jnp.float32)
            out_ref[...] += (both[:width] + both[width:]) + rest
            return carry

        lax.fori_loop(0, info[3], step, 0)

    at = jnp.clip(slot - info[6], 0, chunks - 1)
    for code, ref in enumerate((start_ref, start_rest_ref)):
        @pl.when((info[4] == 1) & (info[10] == code))
        def _(ref=ref):
            out_ref[...] = ref[at] - out_ref[...]

    @pl.when(info[5] == 1)
    def _():
        second[...] = out_ref[...]

    if sent[1]:
        @pl.when(info[7] == 1)
        def _():
            out_ref[...] = side_ref[...]

    keep_line(lambda copy: copy.start())
    keep_line(lambda copy: copy.wait())
    keep_pair(lambda copy: copy.wait())


def advance(slot, info, received, start, start_rest, high, low, store, waited):
    chunks, width, block = start.shape
    sent = tuple(value is not None for value in received)
    operands = [in_vmem(value) for value in received if value is not None]
    operands += [in_vmem(start), in_vmem(start_rest), in_vmem(high), in_vmem(low)]
    count = len(operands)
    extra = list(waited) + ([] if store is None else [in_hbm(store)])

    def kernel(info, *refs):
        slot_kernel(slot, chunks, sent, info, *refs[:count], *refs[-4:])

    return pl.pallas_call(
        kernel,
        out_shape=[vmem_shape((width, block), jnp.float32), vmem_shape((2 * width, block), jnp.float32),
                   hbm_shape((chunks, 2, width, block), jnp.float32)],
        in_specs=[pl.BlockSpec(memory_space=pltpu.SMEM)] + [pl.BlockSpec(memory_space=pltpu.VMEM)] * count
        + [pl.BlockSpec(memory_space=pl.ANY)] * len(extra),
        out_specs=[pl.BlockSpec(memory_space=pltpu.VMEM)] * 2 + [pl.BlockSpec(memory_space=pl.ANY)],
        scratch_shapes=[pltpu.SemaphoreType.DMA((2,))],
        input_output_aliases={} if store is None else {count + len(extra): 2},
        compiler_params=pltpu.CompilerParams(vmem_limit_bytes=16 << 20),
        cost_estimate=pl.CostEstimate(
            flops=6 * width * block * high.shape[0], bytes_accessed=32 * width * block, transcendentals=0),
    )(info, *operands, *extra)


def fetch(first_chunk, info, store, arrays, waited):
    _, _, width, block = store.shape
    counts = [len(group) for group in arrays]
    flat_arrays = [array for group in arrays for array in group]

    def kernel(info, store_ref, *refs):
        out_ref, sem = refs[-2:]

        def copies(action):
            for index in range(len(arrays)):
                @pl.when(info[1 + index] == 0)
                def _(index=index):
                    action(pltpu.make_async_copy(store_ref.at[first_chunk + index, info[0]],
                                                 out_ref.at[pl.ds(index * width, width)], sem.at[index]))

        copies(lambda copy: copy.start())
        left = list(refs[:len(flat_arrays)])
        for index, count in enumerate(counts):
            for place in range(count):
                ref = left.pop(0)

                @pl.when(info[1 + index] == place + 1)
                def _(index=index, ref=ref):
                    out_ref[pl.ds(index * width, width)] = ref[...]
        copies(lambda copy: copy.wait())

    return pl.pallas_call(
        kernel,
        out_shape=vmem_shape((len(arrays) * width, block), jnp.float32),
        in_specs=[pl.BlockSpec(memory_space=pltpu.SMEM), pl.BlockSpec(memory_space=pl.ANY)]
        + [pl.BlockSpec(memory_space=pltpu.VMEM)] * len(flat_arrays) + [pl.BlockSpec(memory_space=pl.ANY)] * len(waited),
        out_specs=pl.BlockSpec(memory_space=pltpu.VMEM),
        scratch_shapes=[pltpu.SemaphoreType.DMA((len(arrays),))],
        compiler_params=pltpu.CompilerParams(vmem_limit_bytes=16 << 20),
        cost_estimate=pl.CostEstimate(flops=0, bytes_accessed=0, transcendentals=0),
    )(info, in_hbm(store), *map(in_vmem, flat_arrays), *waited)


def solved_shares(info, store, shares):
    chunks, _, width, block = store.shape
    size = block // shares

    def kernel(info, store_ref, *refs):
        outs, sem = refs[:-1], refs[-1]

        def copies(action):
            for chunk in range(chunks):
                for turn in range(shares):
                    columns = pl.ds(pl.multiple_of(info[1 + turn] * size, size), size)
                    action(pltpu.make_async_copy(store_ref.at[chunk, info[0], :, columns],
                                                 outs[turn].at[pl.ds(chunk * width, width)], sem.at[chunk, turn]))

        copies(lambda copy: copy.start())
        copies(lambda copy: copy.wait())

    return pl.pallas_call(
        kernel,
        out_shape=[vmem_shape((chunks * width, size), jnp.float32)] * shares,
        in_specs=[pl.BlockSpec(memory_space=pltpu.SMEM), pl.BlockSpec(memory_space=pl.ANY)],
        out_specs=[pl.BlockSpec(memory_space=pltpu.VMEM)] * shares,
        scratch_shapes=[pltpu.SemaphoreType.DMA((chunks, shares))],
        compiler_params=pltpu.CompilerParams(vmem_limit_bytes=16 << 20),
        cost_estimate=pl.CostEstimate(flops=0, bytes_accessed=0, transcendentals=0),
    )(info, in_hbm(store))


def turn_kernel(info, chunks, width, store_ref, *refs):
    pairs = chunks // 2
    lines, crossed, series_ref = refs[:pairs], refs[pairs:2 * pairs], refs[2 * pairs]
    both, side_high, side_low, raw, side, sem = refs[-6:]
    block = raw.shape[2]
    dates = series_ref.shape[0]
    total = chunks * width

    def copies(action):
        for chunk in range(chunks):
            rows = pl.ds(chunk * width, width)

            @pl.when(info[0] == 1)
            def _(chunk=chunk, rows=rows):
                for stream in range(2):
                    action(pltpu.make_async_copy(
                        store_ref.at[chunk, stream], raw.at[stream, rows], sem.at[2 * chunk + stream]))

        for pair in range(pairs):
            rows = pl.ds(2 * pair * width, 2 * width)

            @pl.when(info[0] == 0)
            def _(pair=pair, rows=rows):
                action(pltpu.make_async_copy(lines[pair], raw.at[info[1], rows], sem.at[2 * pair]))
                action(pltpu.make_async_copy(crossed[pair], raw.at[1 - info[1], rows], sem.at[2 * pair + 1]))

    copies(lambda copy: copy.start())
    lanes = side.shape[0]
    side[...] = jnp.zeros_like(side)
    side[pl.ds(0, dates)] = series_ref[...]
    first, second = halves(side[...].T)
    side_high[...] = first
    side_low[...] = second
    raw[:, pl.ds(total, lanes - total)] = jnp.zeros((2, lanes - total, block), jnp.float32)
    copies(lambda copy: copy.wait())
    for stream in range(2):
        first, second = halves(raw[stream].T)
        both[pl.ds(stream * block, block), pl.ds(0, lanes)] = first
        both[pl.ds(stream * block, block), pl.ds(lanes, lanes)] = second


def turned(info, store, sources, series, waited):
    chunks, _, width, block = store.shape
    dates, points = series.shape
    lanes = -(-max(dates, chunks * width) // 128) * 128
    count = 2 + len(sources)

    def kernel(info, *refs):
        turn_kernel(info, chunks, width, *refs[:count], *refs[count + len(waited):])

    whole = pl.BlockSpec(memory_space=pltpu.VMEM)
    solved = vmem_shape((2 * block, 2 * lanes), jnp.bfloat16)
    side = vmem_shape((points, lanes), jnp.bfloat16)
    return pl.pallas_call(
        kernel,
        out_shape=[solved, side, side],
        in_specs=[pl.BlockSpec(memory_space=pltpu.SMEM)] + [pl.BlockSpec(memory_space=pl.ANY)] * (1 + len(sources))
        + [whole] + [pl.BlockSpec(memory_space=pl.ANY)] * len(waited),
        out_specs=[whole] * 3,
        scratch_shapes=[
            pltpu.VMEM((2, lanes, block), jnp.float32),
            pltpu.VMEM((lanes, points), jnp.float32),
            pltpu.SemaphoreType.DMA((2 * chunks,)),
        ],
        compiler_params=pltpu.CompilerParams(vmem_limit_bytes=16 << 20),
        cost_estimate=pl.CostEstimate(flops=0, bytes_accessed=0, transcendentals=0),
    )(info, in_hbm(store), *sources, in_vmem(series), *waited)


def residual_kernel(info, first_tile, tiles, both, side_high, side_low, place_ref, panel_ref, *rest):
    out_ref, held, sem = rest[-3:]
    steps, rows = held.shape[:2]
    total = out_ref.shape[0]
    per_tile = steps // tiles

    def source_rows(step):
        start = info[2 + first_tile + step // per_tile] * (per_tile * rows) + step % per_tile * rows
        return pl.ds(pl.multiple_of(start, rows), rows)

    def panel_rows(step):
        return pltpu.make_async_copy(panel_ref.at[source_rows(step)], held.at[step], sem.at[step])

    for step in range(steps):
        panel_rows(step).start()

    def multiply(step, carry):
        panel_rows(step).wait()
        factor_high, factor_low = halves(held[step])
        lanes = side_high.shape[1]
        wide = jnp.dot(factor_high, both[...], preferred_element_type=jnp.float32)
        product = ((wide[:, :lanes] + wide[:, lanes:])
                   + jnp.dot(factor_low, both[:, pl.ds(0, lanes)], preferred_element_type=jnp.float32))
        places = lax.broadcasted_iota(jnp.int32, (rows, side_high.shape[0]), 1)
        chosen = jnp.where(places == place_ref[source_rows(step)], 1.0, 0.0).astype(jnp.bfloat16)
        value = (jnp.dot(chosen, side_high[...], preferred_element_type=jnp.float32)
                 + jnp.dot(chosen, side_low[...], preferred_element_type=jnp.float32)) - product
        out_ref[:, pl.ds(pl.multiple_of(step * rows, rows), rows)] = value.T[:total]
        return carry

    lax.fori_loop(0, steps, multiply, 0)


def residual_tiles(info, first_tile, tiles, size, total, parts, place, panel, waited):
    depth = panel.shape[1]
    rows = 256
    steps = tiles * size // rows

    def kernel(info, *refs):
        residual_kernel(info, first_tile, tiles, *refs[:5], *refs[-3:])

    whole = pl.BlockSpec(memory_space=pltpu.VMEM)
    return pl.pallas_call(
        kernel,
        out_shape=vmem_shape((total, tiles * size), jnp.float32),
        in_specs=[pl.BlockSpec(memory_space=pltpu.SMEM)] + [whole] * 4
        + [pl.BlockSpec(memory_space=pl.ANY)] * (1 + len(waited)),
        out_specs=whole,
        scratch_shapes=[pltpu.VMEM((steps, rows, depth), jnp.float32), pltpu.SemaphoreType.DMA((steps,))],
        compiler_params=pltpu.CompilerParams(vmem_limit_bytes=36 << 20),
        cost_estimate=pl.CostEstimate(
            flops=6 * total * tiles * size * depth, bytes_accessed=4 * tiles * size * depth, transcendentals=0),
    )(info, *map(in_vmem, parts), in_vmem(place), in_hbm(panel), *waited)


def add_kernel(left_ref, right_ref, out_ref):
    out_ref[...] = left_ref[...] + right_ref[:, pl.ds(0, out_ref.shape[1])]


def added(left, right):
    whole = pl.BlockSpec(memory_space=pltpu.VMEM)
    return pl.pallas_call(
        add_kernel,
        out_shape=vmem_shape(left.shape, left.dtype),
        in_specs=[whole] * 2,
        out_specs=whole,
        compiler_params=pltpu.CompilerParams(vmem_limit_bytes=16 << 20),
    )(in_vmem(left), in_vmem(right))


def make_line_body(row_count, col_count):
    levels = row_count // 2
    chunks = LINE_CHUNKS

    def flat(level, side, col):
        return (2 * level + side) * col_count + col

    def body(series, point_order, step_block, panel, diag_inverse):
        f32 = jnp.float32
        dates, own_points = series.shape
        block = diag_inverse.shape[1]
        group_rows, depth = panel.shape
        local_blocks = group_rows // block
        width = -(-dates // (16 * chunks)) * 16
        padded = width * chunks
        row = lax.axis_index("rows")
        col = lax.axis_index("cols")
        level, side = row // 2, row % 2

        def send(value, pairs):
            return lax.ppermute(value, ("rows", "cols"), pairs)

        def solver(step):
            return flat(step // 2, step % 2, max(step - 1, 0) // 2)

        def busy(start, slot):
            return 0 <= slot - start < chunks

        above, same = level > col, level == col
        second_solver = same & (side == 1)
        last = (side == 0) & (level == col + 1)
        origin = (row == 0) & (col == 0)
        is_solver = second_solver | last | origin

        shares = [series]
        for turn in range(1, col_count):
            pairs = []
            for step in range(STEPS):
                here = max(step - 1, 0) // 2
                pairs.append((flat(step // 2, step % 2, (here + turn) % col_count), flat(step // 2, step % 2, here)))
            shares.append(send(series, pairs))

        per_tile = 256
        top = levels - 1
        last_factor = jnp.where(above, depth // per_tile - 1, jnp.where(second_solver, block // per_tile - 1, 0))
        slot_index = step_block[row] % local_blocks
        local_order = point_order % group_rows
        block_order = lax.dynamic_slice(local_order, (slot_index * block,), (block,))
        place = (block_order // own_points - col) % col_count * own_points + block_order % own_points
        first_direct = 2 * top + 2
        arrived = jnp.where(origin, 0, jnp.where((col == top) & (level == top - 1), first_direct, 3 * col - level + 1))
        from_direct = (col == top) & (level < top - 1)
        stored_at = jnp.where(above, level + col + 1, jnp.where(from_direct, first_direct + 4 * chunks, arrived))
        own_place = jnp.where(local_order // own_points != col, -1, local_order % own_points)[:, None]
        def pack(*values):
            return jnp.stack([jnp.asarray(value).astype(jnp.int32) for value in values])

        factor_info = pack(slot_index, last_factor)
        start_info = pack(slot_index, origin)
        rest_info = pack(slot_index, is_solver & jnp.logical_not(origin))
        slot_info = pack(
            (above | second_solver) & (col > 0),
            jnp.where(above, 2, jnp.where(second_solver, 1, 0)),
            last,
            jnp.where(above, depth // TILE, jnp.where(second_solver, block // TILE, 0)),
            is_solver,
            second_solver,
            jnp.where(origin, 0, level + col + 1),
            jnp.logical_not(above | second_solver | origin),
            stored_at,
            side,
            jnp.logical_not(origin),
        )
        usual = jnp.where(from_direct, level + 1, 0)
        fetch_info = pack(side, usual, usual)
        late_info = pack(side, usual, jnp.where((col == top) & (level == top - 1), top, usual))
        solved_info = pack(side, *[(col + turn) % col_count for turn in range(col_count)])
        residual_info = pack(above, side, col ^ 3, col ^ 1, col ^ 2, col)
        place = place[None, :]
        waited = [place, start_info, rest_info, slot_info, fetch_info, late_info, solved_info, residual_info, own_place]

        high, low = chain_factors(factor_info, diag_inverse, panel, per_tile, waited)
        start = start_values(start_info, shares, place, diag_inverse, chunks, width, [])

        chain_pairs = [(solver(step), solver(step + 1)) for step in range(STEPS - 1)]
        side_pairs = [(0, 0)]
        down_pairs, cross_pairs = [], []
        for c in range(col_count):
            for z in range(levels):
                for y in range(2):
                    if z > c:
                        side_pairs.append((flat(z, y, c), flat(z, y, c + 1)))
                        continue
                    cross_pairs.append((flat(z, y, c), flat(z, 1 - y, c)))
                    if z and (c < levels - 1 or z == c):
                        down_pairs.append((flat(z, y, c), flat(z - 1, y, c)))
        direct_pairs = [[(flat(top, y, top), flat(z, y, top)) for y in range(2)] for z in range(top)]
        late_pairs = direct_pairs[top - 1]
        mine, crossed, direct = [], [], []

        def send_direct():
            direct.append([send(out, direct_pairs[z]) for z in range(top - 1)])

        def cross(info, arrays, waited):
            mine.append(fetch(2 * len(mine), info, store, arrays, mine[-1:] + waited))
            crossed.append(send(mine[-1], cross_pairs))

        out = pair = store = None
        start_rest = start
        last_solve = STEPS - 1 + chunks - 1
        for slot in range(last_solve + 1):
            received = [None, None, None]
            if slot:
                ups = [(flat(z, y, c), flat(z + 1, y, c)) for c in range(col_count) for z in range(c, levels - 1)
                       for y in range(2) if busy(z + c + 1, slot - 1)]
                received = [send(out, chain_pairs), send(out, side_pairs + down_pairs),
                            send(pair, ups) if ups else None]
            if slot >= first_direct:
                send_direct()
            out, pair, store = advance(slot, slot_info, received, start, start_rest, high, low, store,
                                       mine[-1:] + (direct[-2] if len(direct) > 1 else []))
            if slot == 0:
                start_rest = start_values(rest_info, shares, place, diag_inverse, chunks, width, [out])
            if slot == first_direct + 1:
                cross(fetch_info, direct, [])

        send_direct()
        late = send(out, late_pairs)
        pieces = solved_shares(solved_info, store, col_count)
        delivered = []
        for turn in range(1, col_count):
            pairs = [(flat(z, y, z), flat(z, y, (z + turn) % col_count)) for z in range(levels) for y in range(2)]
            delivered.append(send(pieces[turn], pairs))
        cross(late_info, [direct[-2], direct[-1] + [late]], [pieces[0]])
        near = [(at * col_count + here, at * col_count + (here ^ 1))
                for at in range(row_count) for here in range(col_count)]
        far = [(at * col_count + here, at * col_count + (here ^ 2))
               for at in range(row_count) for here in range(col_count)]

        size = group_rows // col_count
        parts = turned(residual_info, store, mine + crossed, series, delivered)
        def share(tile, waited):
            return residual_tiles(residual_info, tile, 1, size, padded, parts, own_place, panel, waited)

        first_give = share(0, [])
        moved_first = send(first_give, near)
        passed = added(share(2, [first_give]), moved_first)
        moved_far = send(passed, far)
        give = share(1, [passed])
        moved = send(give, near)
        own = share(3, [give, moved_far])
        solved = pieces[0]
        for turn in range(1, col_count):
            solved = jnp.where((col - level) % col_count == turn, delivered[turn - 1], solved)

        residual = ((own + moved) + moved_far)[:dates]
        return solved[:dates].T, residual.T

    return body


def make_body(row_count, col_count):
    base = row_count - STEPS

    def body(series, point_order, step_block, panel, diag_inverse):
        f32 = jnp.float32
        dates, own_points = series.shape
        block = diag_inverse.shape[1]
        group_rows = panel.shape[0]
        local_blocks = group_rows // block
        per = panel.shape[1] // block
        width = -(-dates // (8 * CHUNKS)) * 8
        padded = width * CHUNKS

        def column(step):
            return step // per

        solver_col = [0] + [column(step - 1) for step in range(1, STEPS)]

        def arrival(start, distance):
            if distance >= 1:
                return start + -(-distance // 2)
            return start + 1 + (-distance) // 2

        def fits(hop):
            for step in range(STEPS):
                for earlier in range(step):
                    due = hop * step - (solver_col[step] - column(earlier))
                    if arrival(hop * earlier, step - earlier) > due:
                        return False
            return True

        hop = 1
        while not fits(hop):
            hop += 1

        def flat(row, col):
            return row * col_count + col

        def busy(start, slot):
            return 0 <= slot - start < CHUNKS

        row = lax.axis_index("rows")
        col = lax.axis_index("cols")
        step_here = row - base
        has_step = step_here >= 0
        step_safe = jnp.maximum(step_here, 0)
        solver_here = jnp.where(step_safe == 0, 0, (step_safe - 1) // per)
        is_solver = has_step & (col == solver_here)

        def send(value, pairs):
            return lax.ppermute(value, ("rows", "cols"), pairs)

        first_row = step_block[step_safe] % local_blocks * block
        inverse = lax.dynamic_slice(diag_inverse, (first_row, jnp.int32(0)), (block, block))
        factor = lax.dynamic_slice(panel, (first_row, jnp.int32(0)), (block, per * block))
        chain_factor = lax.dot_general(
            factor, inverse, (((0,), (1,)), ((), ())),
            precision=lax.Precision.HIGH, preferred_element_type=f32)

        shares = [series]
        for turn in range(1, col_count):
            pairs = [
                (flat(base + step, (solver_col[step] + turn) % col_count), flat(base + step, solver_col[step]))
                for step in range(STEPS)
            ]
            shares.append(send(series, pairs))
        gathered = jnp.concatenate(shares, axis=1)
        local_order = point_order % group_rows

        block_order = lax.dynamic_slice(local_order, (first_row,), (block,))
        place = (block_order // own_points - col) % col_count * own_points + block_order % own_points
        side = picked(gathered, place)
        start_value = lax.dot_general(
            side, inverse, (((1,), (1,)), ((), ())),
            precision=lax.Precision.HIGH, preferred_element_type=f32)
        start_value = jnp.pad(start_value, ((0, padded - dates), (0, 0))).reshape(CHUNKS, width, block)

        zero = jnp.zeros((width, block), f32)
        held = [jnp.zeros((CHUNKS + 1, width, block), f32) for _ in range(per)]
        latest = [zero] * per
        outgoing = None
        streams = [col * per + index for index in range(per)]
        gaps = [step_here - stream for stream in streams]
        starts = [hop * stream for stream in streams]

        def arrival_here(start, gap):
            return jnp.where(gap >= 1, start + (gap + 1) // 2, start + 1 + (-gap) // 2)

        arrivals = [arrival_here(start, gap) for start, gap in zip(starts, gaps)]
        due = hop * step_here - (solver_here - col)

        def pick_chunk(values, chunk):
            return lax.dynamic_index_in_dim(values, jnp.clip(chunk, 0, CHUNKS - 1), 0, keepdims=False)

        last_slot = max(arrival(hop * step, place_row - base - step)
                        for step in range(STEPS) for place_row in range(row_count)) + CHUNKS - 1
        for slot in range(last_slot + 1):
            before = slot - 1
            one_up, two_up, level, one_down, added = [], [], [], [], []
            if before >= 0:
                for step in range(STEPS):
                    source = flat(base + step, solver_col[step])
                    if busy(hop * step, before):
                        if step + 1 < STEPS:
                            one_up.append((source, flat(base + step + 1, column(step))))
                        if step + 2 < STEPS:
                            two_up.append((source, flat(base + step + 2, column(step))))
                        if solver_col[step] != column(step):
                            level.append((source, flat(base + step, column(step))))
                        if base + step >= 1:
                            one_down.append((source, flat(base + step - 1, column(step))))
                    for from_col in range(solver_col[step]):
                        if busy(hop * step - (solver_col[step] - from_col), before):
                            added.append((flat(base + step, from_col), flat(base + step, from_col + 1)))
            from_one_up = send(outgoing, one_up) if one_up else zero
            incoming = send(outgoing, added) if added else zero
            from_two_up = send(outgoing, two_up) if two_up else zero
            from_level = send(outgoing, level) if level else zero
            from_one_down = send(outgoing, one_down) if one_down else zero
            received_up, received_down = [], []
            for index in range(per):
                upward, downward = [], []
                for stream in range(index, STEPS, per):
                    for at in range(row_count):
                        gap = at - base - stream
                        if busy(arrival(hop * stream, gap), before):
                            if gap >= 1 and at + 2 < row_count:
                                upward.append((flat(at, column(stream)), flat(at + 2, column(stream))))
                            if gap <= 0 and at >= 2:
                                downward.append((flat(at, column(stream)), flat(at - 2, column(stream))))
                received_up.append(send(latest[index], upward) if upward else zero)
                received_down.append(send(latest[index], downward) if downward else zero)

            inputs = []
            for index in range(per):
                gap = gaps[index]
                up = jnp.where(gap == 1, from_one_up, jnp.where(gap == 2, from_two_up, received_up[index]))
                same = jnp.where(col == solver_here, zero if outgoing is None else outgoing, from_level)
                down = jnp.where(gap == 0, same, jnp.where(gap == -1, from_one_down, received_down[index]))
                got = jnp.where(gap >= 1, up, down)
                chunk = slot - arrivals[index]
                valid = (chunk >= 0) & (chunk < CHUNKS)
                needed = slot - due
                ready = jnp.where(needed == chunk, up, pick_chunk(held[index], needed))
                inputs.append(jnp.where((gap >= 1) & has_step, ready, 0))
                held[index] = lax.dynamic_update_index_in_dim(
                    held[index], got, jnp.where(valid, chunk, CHUNKS), 0)
                latest[index] = got
            if slot <= hop * (STEPS - 1) + CHUNKS - 1:
                total = incoming + jnp.dot(
                    jnp.concatenate(inputs, axis=1), chain_factor,
                    precision=lax.Precision.HIGH, preferred_element_type=f32)
                outgoing = jnp.where(is_solver, pick_chunk(start_value, slot - due) - total, total)

        whole = [values[:CHUNKS].reshape(padded, block)[:dates] for values in held]
        out_rows = STEPS * block // (row_count * col_count)

        def wanted(at):
            return at * col_count * out_rows // block

        source_col = row * col_count * out_rows // block // per
        stream_index = row * col_count * out_rows // block % per
        chosen = whole[0]
        for index in range(1, per):
            chosen = jnp.where(stream_index == index, whole[index], chosen)

        def piece(target):
            first = (row * col_count + target) * out_rows % block
            return lax.dynamic_slice(chosen, (jnp.int32(0), first), (dates, out_rows))

        solved = piece(col)
        for turn in range(1, col_count):
            pairs = [
                (flat(at, column(wanted(at))), flat(at, (column(wanted(at)) + turn) % col_count))
                for at in range(row_count)
            ]
            moved = send(piece((col + turn) % col_count), pairs)
            solved = jnp.where((col - source_col) % col_count == turn, moved, solved)

        away = local_order // own_points != col
        own_place = jnp.where(away, -1, local_order % own_points)
        product = lax.dot_general(
            jnp.concatenate(whole, axis=1), panel, (((1,), (1,)), ((), ())),
            precision=lax.Precision.HIGH, preferred_element_type=f32)
        left = picked(series, own_place) - product
        distance = 1
        parts = left.reshape(dates, col_count, group_rows // col_count)
        pieces = [parts[:, index] for index in range(col_count)]
        while distance < col_count:
            bit = (col // distance) % 2
            keep, give = [], []
            for index in range(0, len(pieces), 2):
                keep.append(jnp.where(bit == 0, pieces[index], pieces[index + 1]))
                give.append(jnp.where(bit == 0, pieces[index + 1], pieces[index]))
            pairs = [(flat(at, here), flat(at, here ^ distance)) for at in range(row_count) for here in range(col_count)]
            moved = send(jnp.concatenate(give, axis=1) if len(give) > 1 else give[0], pairs)
            size = group_rows // col_count
            pieces = [value + moved[:, index * size:(index + 1) * size] for index, value in enumerate(keep)]
            distance *= 2
        return solved.T, pieces[0].T

    return body


def solution(mesh):
    in_specs = (P(None, ("rows", "cols")), P("rows"), P(), P("rows", "cols"), P("rows", None))
    out_specs = (P(("rows", "cols"), None), P(("rows", "cols"), None))
    row_count, col_count = mesh.shape["rows"], mesh.shape["cols"]
    lines = row_count == STEPS and 2 * col_count == STEPS
    body = (make_line_body if lines else make_body)(row_count, col_count)
    return jax.shard_map(body, mesh=mesh, in_specs=in_specs, out_specs=out_specs, check_vma=False)
```

```python
import jax
import jax.numpy as jnp
from jax import lax
from jax.experimental import pallas as pl
from jax.experimental.pallas import tpu as pltpu
from jax.sharding import PartitionSpec as P

STEPS = 8
CHUNKS = 4
LINE_CHUNKS = 4
TILE = 512


def split_hi(value):
    return lax.reduce_precision(value, 8, 7)


def halves(value):
    high = value.astype(jnp.bfloat16)
    return high, (value - high.astype(jnp.float32)).astype(jnp.bfloat16)


def one_hot(index, depth):
    return (lax.broadcasted_iota(jnp.int32, (depth, index.shape[0]), 0) == index[None, :]).astype(jnp.bfloat16)


def picked(values, index):
    chosen = one_hot(index, values.shape[1])
    high = split_hi(values)
    low = split_hi(values - high)
    return (jnp.dot(high.astype(jnp.bfloat16), chosen, preferred_element_type=jnp.float32)
            + jnp.dot(low.astype(jnp.bfloat16), chosen, preferred_element_type=jnp.float32))


def dot_nt(left, right):
    return lax.dot_general(left, right, (((1,), (1,)), ((), ())), preferred_element_type=jnp.float32)


def in_vmem(value):
    return pltpu.with_memory_space_constraint(value, pltpu.VMEM)


def in_hbm(value):
    return pltpu.with_memory_space_constraint(value, pltpu.HBM)


def vmem_shape(shape, dtype):
    return pltpu.VMEM(shape, dtype)


def hbm_shape(shape, dtype):
    return pltpu.HBM(shape, dtype)


def factor_kernel(info, inverse_ref, panel_ref, *rest):
    high_ref, low_ref, inverse_high, inverse_low = rest[-4:]
    tile = pl.program_id(0)

    @pl.when(tile == 0)
    def _():
        high, low = halves(inverse_ref[...])
        inverse_high[...] = high
        inverse_low[...] = low

    @pl.when(tile <= info[1])
    def _():
        high, low = halves(panel_ref[...])
        value = (jnp.dot(inverse_high[...], high, preferred_element_type=jnp.float32)
                 + jnp.dot(inverse_low[...], high, preferred_element_type=jnp.float32)
                 + jnp.dot(inverse_high[...], low, preferred_element_type=jnp.float32))
        high, low = halves(value.T)
        high_ref[...] = high
        low_ref[...] = low


def chain_factors(info, diag_inverse, panel, tile, waited):
    block = diag_inverse.shape[1]
    depth = panel.shape[1]
    shape = vmem_shape((depth, block), jnp.bfloat16)
    return pl.pallas_call(
        factor_kernel,
        out_shape=[shape, shape],
        grid_spec=pltpu.PrefetchScalarGridSpec(
            num_scalar_prefetch=1,
            grid=(depth // tile,),
            in_specs=[
                pl.BlockSpec((block, block), lambda t, info: (info[0], 0)),
                pl.BlockSpec((block, tile), lambda t, info: (info[0], jnp.minimum(t, info[1]))),
            ] + [pl.BlockSpec(memory_space=pl.ANY)] * len(waited),
            out_specs=[pl.BlockSpec((tile, block), lambda t, info: (jnp.minimum(t, info[1]), 0))] * 2,
            scratch_shapes=[pltpu.VMEM((block, block), jnp.bfloat16)] * 2,
        ),
        compiler_params=pltpu.CompilerParams(vmem_limit_bytes=44 << 20),
        cost_estimate=pl.CostEstimate(
            flops=6 * block * block * depth, bytes_accessed=4 * block * (block + 2 * depth), transcendentals=0),
    )(info, in_hbm(diag_inverse), in_hbm(panel), *waited)


def start_kernel(info, *refs):
    shares, (place_ref, source_ref), (out_ref, inverse_ref, side, high, low, sem) = refs[:-8], refs[-8:-6], refs[-6:]
    dates, points = shares[0].shape
    lanes = high.shape[1]
    chunks, width, block = out_ref.shape
    tile = 256
    steps = block // tile

    @pl.when(info[1] == 1)
    def _():
        def inverse_rows(step):
            rows = pl.ds(pl.multiple_of(step * tile, tile), tile)
            source = pl.ds(pl.multiple_of(info[0] * block + step * tile, tile), tile)
            return pltpu.make_async_copy(source_ref.at[source], inverse_ref.at[rows], sem.at[step])

        for step in range(steps):
            inverse_rows(step).start()
        side[...] = jnp.zeros_like(side)
        for index, share in enumerate(shares):
            columns = pl.ds(index * points, points)
            first, second = halves(share[...])
            side[pl.ds(0, dates), columns] = first
            side[pl.ds(lanes, dates), columns] = second

        def order(step, carry):
            columns = pl.ds(pl.multiple_of(step * tile, tile), tile)
            places = lax.broadcasted_iota(jnp.int32, (side.shape[1], tile), 0)
            chosen = jnp.where(places == place_ref[:, columns], 1.0, 0.0).astype(jnp.bfloat16)
            both = jnp.dot(side[...], chosen, preferred_element_type=jnp.float32)
            first, second = halves((both[:lanes] + both[lanes:]).T)
            high[columns] = first
            low[columns] = second
            return carry

        def multiply(step, carry):
            rows = pl.ds(pl.multiple_of(step * tile, tile), tile)
            inverse_rows(step).wait()
            first, second = halves(inverse_ref[rows])
            value = (jnp.dot(first, high[...], preferred_element_type=jnp.float32)
                     + jnp.dot(second, high[...], preferred_element_type=jnp.float32)
                     + jnp.dot(first, low[...], preferred_element_type=jnp.float32)).T
            for chunk in range(chunks):
                out_ref[chunk, :, rows] = value[chunk * width:(chunk + 1) * width]
            return carry

        lax.fori_loop(0, steps, order, 0)
        lax.fori_loop(0, steps, multiply, 0)


def start_values(info, shares, place, diag_inverse, chunks, width, waited):
    block = diag_inverse.shape[1]
    dates, points = shares[0].shape
    lanes = -(-max(dates, chunks * width) // 128) * 128
    count = len(shares) + 2
    ordered = pltpu.VMEM((block, lanes), jnp.bfloat16)

    def kernel(info, *refs):
        start_kernel(info, *refs[:count], *refs[-6:])

    whole = pl.BlockSpec(memory_space=pltpu.VMEM)
    return pl.pallas_call(
        kernel,
        out_shape=vmem_shape((chunks, width, block), jnp.float32),
        in_specs=[pl.BlockSpec(memory_space=pltpu.SMEM)] + [whole] * (count - 1)
        + [pl.BlockSpec(memory_space=pl.ANY)] * (1 + len(waited)),
        out_specs=whole,
        scratch_shapes=[
            pltpu.VMEM((block, block), jnp.float32),
            pltpu.VMEM((2 * lanes, len(shares) * points), jnp.bfloat16),
            ordered,
            ordered,
            pltpu.SemaphoreType.DMA((block // 256,)),
        ],
        compiler_params=pltpu.CompilerParams(vmem_limit_bytes=28 << 20),
        cost_estimate=pl.CostEstimate(
            flops=10 * dates * block * block, bytes_accessed=4 * block * (block + 2 * dates), transcendentals=0),
    )(info, *map(in_vmem, shares), in_vmem(place), in_hbm(diag_inverse), *waited)


def slot_kernel(slot, chunks, sent, info, *refs):
    refs = list(refs)
    chain_ref = refs.pop(0) if sent[0] else None
    side_ref = refs.pop(0) if sent[1] else None
    up_ref = refs.pop(0) if sent[2] else None
    start_ref, start_rest_ref, high_ref, low_ref, out_ref, pair_ref, store_ref, sem = refs
    width, block = out_ref.shape
    first, second = pair_ref.at[pl.ds(0, width)], pair_ref.at[pl.ds(width, width)]
    chunk = slot - info[8]
    stored = (chunk >= 0) & (chunk < chunks)

    def keep_pair(action):
        @pl.when(stored & (info[1] == 2))
        def _():
            for stream in range(2):
                action(pltpu.make_async_copy(
                    pair_ref.at[pl.ds(stream * width, width)], store_ref.at[chunk, stream], sem.at[stream]))

    def keep_line(action):
        @pl.when(stored & (info[1] != 2))
        def _():
            action(pltpu.make_async_copy(out_ref, store_ref.at[chunk, info[9]], sem.at[0]))

    @pl.when(info[0] == 1)
    def _():
        out_ref[...] = side_ref[...] if sent[1] else jnp.zeros_like(out_ref)

    @pl.when(info[0] == 0)
    def _():
        out_ref[...] = jnp.zeros_like(out_ref)

    for code, ref in enumerate((side_ref, chain_ref, None if up_ref is None else up_ref.at[pl.ds(0, width)])):
        if ref is not None:
            @pl.when(info[1] == code)
            def _(ref=ref):
                first[...] = ref[...]
    for code, ref in enumerate((None if up_ref is None else up_ref.at[pl.ds(width, width)], chain_ref)):
        if ref is not None:
            @pl.when(info[2] == code)
            def _(ref=ref):
                second[...] = ref[...]

    keep_pair(lambda copy: copy.start())

    if any(sent):
        def step(tile, carry):
            per_stream = block // TILE
            rows = pl.ds(pl.multiple_of(tile // per_stream * width, 16), width)
            columns = pl.ds(pl.multiple_of(tile % per_stream * TILE, TILE), TILE)
            factor = pl.ds(pl.multiple_of(tile * TILE, TILE), TILE)
            high, low = halves(pair_ref[rows, columns])
            both = jnp.dot(jnp.concatenate([high, low], axis=0), high_ref[factor], preferred_element_type=jnp.float32)
            rest = jnp.dot(high, low_ref[factor], preferred_element_type=jnp.float32)
            out_ref[...] += (both[:width] + both[width:]) + rest
            return carry

        lax.fori_loop(0, info[3], step, 0)

    at = jnp.clip(slot - info[6], 0, chunks - 1)
    for code, ref in enumerate((start_ref, start_rest_ref)):
        @pl.when((info[4] == 1) & (info[10] == code))
        def _(ref=ref):
            out_ref[...] = ref[at] - out_ref[...]

    @pl.when(info[5] == 1)
    def _():
        second[...] = out_ref[...]

    if sent[1]:
        @pl.when(info[7] == 1)
        def _():
            out_ref[...] = side_ref[...]

    keep_line(lambda copy: copy.start())
    keep_line(lambda copy: copy.wait())
    keep_pair(lambda copy: copy.wait())


def advance(slot, info, received, start, start_rest, high, low, store, waited):
    chunks, width, block = start.shape
    sent = tuple(value is not None for value in received)
    operands = [in_vmem(value) for value in received if value is not None]
    operands += [in_vmem(start), in_vmem(start_rest), in_vmem(high), in_vmem(low)]
    count = len(operands)
    extra = list(waited) + ([] if store is None else [in_hbm(store)])

    def kernel(info, *refs):
        slot_kernel(slot, chunks, sent, info, *refs[:count], *refs[-4:])

    return pl.pallas_call(
        kernel,
        out_shape=[vmem_shape((width, block), jnp.float32), vmem_shape((2 * width, block), jnp.float32),
                   hbm_shape((chunks, 2, width, block), jnp.float32)],
        in_specs=[pl.BlockSpec(memory_space=pltpu.SMEM)] + [pl.BlockSpec(memory_space=pltpu.VMEM)] * count
        + [pl.BlockSpec(memory_space=pl.ANY)] * len(extra),
        out_specs=[pl.BlockSpec(memory_space=pltpu.VMEM)] * 2 + [pl.BlockSpec(memory_space=pl.ANY)],
        scratch_shapes=[pltpu.SemaphoreType.DMA((2,))],
        input_output_aliases={} if store is None else {count + len(extra): 2},
        compiler_params=pltpu.CompilerParams(vmem_limit_bytes=16 << 20),
        cost_estimate=pl.CostEstimate(
            flops=6 * width * block * high.shape[0], bytes_accessed=32 * width * block, transcendentals=0),
    )(info, *operands, *extra)


def fetch(first_chunk, info, store, arrays, waited):
    _, _, width, block = store.shape
    counts = [len(group) for group in arrays]
    flat_arrays = [array for group in arrays for array in group]

    def kernel(info, store_ref, *refs):
        out_ref, sem = refs[-2:]

        def copies(action):
            for index in range(len(arrays)):
                @pl.when(info[1 + index] == 0)
                def _(index=index):
                    action(pltpu.make_async_copy(store_ref.at[first_chunk + index, info[0]],
                                                 out_ref.at[pl.ds(index * width, width)], sem.at[index]))

        copies(lambda copy: copy.start())
        left = list(refs[:len(flat_arrays)])
        for index, count in enumerate(counts):
            for place in range(count):
                ref = left.pop(0)

                @pl.when(info[1 + index] == place + 1)
                def _(index=index, ref=ref):
                    out_ref[pl.ds(index * width, width)] = ref[...]
        copies(lambda copy: copy.wait())

    return pl.pallas_call(
        kernel,
        out_shape=vmem_shape((len(arrays) * width, block), jnp.float32),
        in_specs=[pl.BlockSpec(memory_space=pltpu.SMEM), pl.BlockSpec(memory_space=pl.ANY)]
        + [pl.BlockSpec(memory_space=pltpu.VMEM)] * len(flat_arrays) + [pl.BlockSpec(memory_space=pl.ANY)] * len(waited),
        out_specs=pl.BlockSpec(memory_space=pltpu.VMEM),
        scratch_shapes=[pltpu.SemaphoreType.DMA((len(arrays),))],
        compiler_params=pltpu.CompilerParams(vmem_limit_bytes=16 << 20),
        cost_estimate=pl.CostEstimate(flops=0, bytes_accessed=0, transcendentals=0),
    )(info, in_hbm(store), *map(in_vmem, flat_arrays), *waited)


def solved_shares(info, store, shares):
    chunks, _, width, block = store.shape
    size = block // shares

    def kernel(info, store_ref, *refs):
        outs, sem = refs[:-1], refs[-1]

        def copies(action):
            for chunk in range(chunks):
                for turn in range(shares):
                    columns = pl.ds(pl.multiple_of(info[1 + turn] * size, size), size)
                    action(pltpu.make_async_copy(store_ref.at[chunk, info[0], :, columns],
                                                 outs[turn].at[pl.ds(chunk * width, width)], sem.at[chunk, turn]))

        copies(lambda copy: copy.start())
        copies(lambda copy: copy.wait())

    return pl.pallas_call(
        kernel,
        out_shape=[vmem_shape((chunks * width, size), jnp.float32)] * shares,
        in_specs=[pl.BlockSpec(memory_space=pltpu.SMEM), pl.BlockSpec(memory_space=pl.ANY)],
        out_specs=[pl.BlockSpec(memory_space=pltpu.VMEM)] * shares,
        scratch_shapes=[pltpu.SemaphoreType.DMA((chunks, shares))],
        compiler_params=pltpu.CompilerParams(vmem_limit_bytes=16 << 20),
        cost_estimate=pl.CostEstimate(flops=0, bytes_accessed=0, transcendentals=0),
    )(info, in_hbm(store))


def turn_kernel(info, chunks, width, store_ref, *refs):
    pairs = chunks // 2
    lines, crossed, series_ref = refs[:pairs], refs[pairs:2 * pairs], refs[2 * pairs]
    both, side_high, side_low, raw, side, sem = refs[-6:]
    block = raw.shape[2]
    dates = series_ref.shape[0]
    total = chunks * width

    def copies(action):
        for chunk in range(chunks):
            rows = pl.ds(chunk * width, width)

            @pl.when(info[0] == 1)
            def _(chunk=chunk, rows=rows):
                for stream in range(2):
                    action(pltpu.make_async_copy(
                        store_ref.at[chunk, stream], raw.at[stream, rows], sem.at[2 * chunk + stream]))

        for pair in range(pairs):
            rows = pl.ds(2 * pair * width, 2 * width)

            @pl.when(info[0] == 0)
            def _(pair=pair, rows=rows):
                action(pltpu.make_async_copy(lines[pair], raw.at[info[1], rows], sem.at[2 * pair]))
                action(pltpu.make_async_copy(crossed[pair], raw.at[1 - info[1], rows], sem.at[2 * pair + 1]))

    copies(lambda copy: copy.start())
    lanes = side.shape[0]
    side[...] = jnp.zeros_like(side)
    side[pl.ds(0, dates)] = series_ref[...]
    first, second = halves(side[...].T)
    side_high[...] = first
    side_low[...] = second
    raw[:, pl.ds(total, lanes - total)] = jnp.zeros((2, lanes - total, block), jnp.float32)
    copies(lambda copy: copy.wait())
    for stream in range(2):
        first, second = halves(raw[stream].T)
        both[pl.ds(stream * block, block), pl.ds(0, lanes)] = first
        both[pl.ds(stream * block, block), pl.ds(lanes, lanes)] = second


def turned(info, store, sources, series, waited):
    chunks, _, width, block = store.shape
    dates, points = series.shape
    lanes = -(-max(dates, chunks * width) // 128) * 128
    count = 2 + len(sources)

    def kernel(info, *refs):
        turn_kernel(info, chunks, width, *refs[:count], *refs[count + len(waited):])

    whole = pl.BlockSpec(memory_space=pltpu.VMEM)
    solved = vmem_shape((2 * block, 2 * lanes), jnp.bfloat16)
    side = vmem_shape((points, lanes), jnp.bfloat16)
    return pl.pallas_call(
        kernel,
        out_shape=[solved, side, side],
        in_specs=[pl.BlockSpec(memory_space=pltpu.SMEM)] + [pl.BlockSpec(memory_space=pl.ANY)] * (1 + len(sources))
        + [whole] + [pl.BlockSpec(memory_space=pl.ANY)] * len(waited),
        out_specs=[whole] * 3,
        scratch_shapes=[
            pltpu.VMEM((2, lanes, block), jnp.float32),
            pltpu.VMEM((lanes, points), jnp.float32),
            pltpu.SemaphoreType.DMA((2 * chunks,)),
        ],
        compiler_params=pltpu.CompilerParams(vmem_limit_bytes=16 << 20),
        cost_estimate=pl.CostEstimate(flops=0, bytes_accessed=0, transcendentals=0),
    )(info, in_hbm(store), *sources, in_vmem(series), *waited)


def residual_kernel(info, first_tile, tiles, both, side_high, side_low, place_ref, panel_ref, *rest):
    out_ref, held, sem = rest[-3:]
    steps, rows = held.shape[:2]
    total = out_ref.shape[0]
    per_tile = steps // tiles

    def source_rows(step):
        start = info[2 + first_tile + step // per_tile] * (per_tile * rows) + step % per_tile * rows
        return pl.ds(pl.multiple_of(start, rows), rows)

    def panel_rows(step):
        return pltpu.make_async_copy(panel_ref.at[source_rows(step)], held.at[step], sem.at[step])

    for step in range(steps):
        panel_rows(step).start()

    def multiply(step, carry):
        panel_rows(step).wait()
        factor_high, factor_low = halves(held[step])
        lanes = side_high.shape[1]
        wide = jnp.dot(factor_high, both[...], preferred_element_type=jnp.float32)
        product = ((wide[:, :lanes] + wide[:, lanes:])
                   + jnp.dot(factor_low, both[:, pl.ds(0, lanes)], preferred_element_type=jnp.float32))
        places = lax.broadcasted_iota(jnp.int32, (rows, side_high.shape[0]), 1)
        chosen = jnp.where(places == place_ref[source_rows(step)], 1.0, 0.0).astype(jnp.bfloat16)
        value = (jnp.dot(chosen, side_high[...], preferred_element_type=jnp.float32)
                 + jnp.dot(chosen, side_low[...], preferred_element_type=jnp.float32)) - product
        out_ref[:, pl.ds(pl.multiple_of(step * rows, rows), rows)] = value.T[:total]
        return carry

    lax.fori_loop(0, steps, multiply, 0)


def residual_tiles(info, first_tile, tiles, size, total, parts, place, panel, waited):
    depth = panel.shape[1]
    rows = 256
    steps = tiles * size // rows

    def kernel(info, *refs):
        residual_kernel(info, first_tile, tiles, *refs[:5], *refs[-3:])

    whole = pl.BlockSpec(memory_space=pltpu.VMEM)
    return pl.pallas_call(
        kernel,
        out_shape=vmem_shape((total, tiles * size), jnp.float32),
        in_specs=[pl.BlockSpec(memory_space=pltpu.SMEM)] + [whole] * 4
        + [pl.BlockSpec(memory_space=pl.ANY)] * (1 + len(waited)),
        out_specs=whole,
        scratch_shapes=[pltpu.VMEM((steps, rows, depth), jnp.float32), pltpu.SemaphoreType.DMA((steps,))],
        compiler_params=pltpu.CompilerParams(vmem_limit_bytes=36 << 20),
        cost_estimate=pl.CostEstimate(
            flops=6 * total * tiles * size * depth, bytes_accessed=4 * tiles * size * depth, transcendentals=0),
    )(info, *map(in_vmem, parts), in_vmem(place), in_hbm(panel), *waited)


def solved_rows(info, shares, dates):
    def kernel(info, *refs):
        for index, ref in enumerate(refs[:-1]):
            @pl.when(info[0] == index)
            def _(ref=ref):
                refs[-1][...] = ref[pl.ds(0, dates)]

    whole = pl.BlockSpec(memory_space=pltpu.VMEM)
    return pl.pallas_call(
        kernel,
        out_shape=jax.ShapeDtypeStruct((dates, shares[0].shape[1]), jnp.float32),
        in_specs=[pl.BlockSpec(memory_space=pltpu.SMEM)] + [whole] * len(shares),
        out_specs=whole,
        compiler_params=pltpu.CompilerParams(vmem_limit_bytes=16 << 20),
    )(info, *map(in_vmem, shares))


def add_kernel(left_ref, right_ref, out_ref):
    out_ref[...] = left_ref[...] + right_ref[:, pl.ds(0, out_ref.shape[1])]


def added(left, right):
    whole = pl.BlockSpec(memory_space=pltpu.VMEM)
    return pl.pallas_call(
        add_kernel,
        out_shape=vmem_shape(left.shape, left.dtype),
        in_specs=[whole] * 2,
        out_specs=whole,
        compiler_params=pltpu.CompilerParams(vmem_limit_bytes=16 << 20),
    )(in_vmem(left), in_vmem(right))


def make_line_body(row_count, col_count):
    levels = row_count // 2
    chunks = LINE_CHUNKS

    def flat(level, side, col):
        return (2 * level + side) * col_count + col

    def body(series, point_order, step_block, panel, diag_inverse):
        f32 = jnp.float32
        dates, own_points = series.shape
        block = diag_inverse.shape[1]
        group_rows, depth = panel.shape
        local_blocks = group_rows // block
        width = -(-dates // (16 * chunks)) * 16
        padded = width * chunks
        row = lax.axis_index("rows")
        col = lax.axis_index("cols")
        level, side = row // 2, row % 2

        def send(value, pairs):
            return lax.ppermute(value, ("rows", "cols"), pairs)

        def solver(step):
            return flat(step // 2, step % 2, max(step - 1, 0) // 2)

        def busy(start, slot):
            return 0 <= slot - start < chunks

        above, same = level > col, level == col
        second_solver = same & (side == 1)
        last = (side == 0) & (level == col + 1)
        origin = (row == 0) & (col == 0)
        is_solver = second_solver | last | origin

        shares = [series]
        for turn in range(1, col_count):
            pairs = []
            for step in range(STEPS):
                here = max(step - 1, 0) // 2
                pairs.append((flat(step // 2, step % 2, (here + turn) % col_count), flat(step // 2, step % 2, here)))
            shares.append(send(series, pairs))

        per_tile = 256
        top = levels - 1
        last_factor = jnp.where(above, depth // per_tile - 1, jnp.where(second_solver, block // per_tile - 1, 0))
        slot_index = step_block[row] % local_blocks
        local_order = point_order % group_rows
        block_order = lax.dynamic_slice(local_order, (slot_index * block,), (block,))
        place = (block_order // own_points - col) % col_count * own_points + block_order % own_points
        arrived = jnp.where(origin, 0, 3 * col - level + 1)
        stored_at = jnp.where(above, level + col + 1, arrived)
        own_place = jnp.where(local_order // own_points != col, -1, local_order % own_points)[:, None]
        def pack(*values):
            return jnp.stack([jnp.asarray(value).astype(jnp.int32) for value in values])

        factor_info = pack(slot_index, last_factor)
        start_info = pack(slot_index, origin)
        rest_info = pack(slot_index, is_solver & jnp.logical_not(origin))
        slot_info = pack(
            (above | second_solver) & (col > 0),
            jnp.where(above, 2, jnp.where(second_solver, 1, 0)),
            last,
            jnp.where(above, depth // TILE, jnp.where(second_solver, block // TILE, 0)),
            is_solver,
            second_solver,
            jnp.where(origin, 0, level + col + 1),
            jnp.logical_not(above | second_solver | origin),
            stored_at,
            side,
            jnp.logical_not(origin),
        )
        late_at = jnp.where((col == top) & (level < top), arrived - (STEPS - 1 + chunks - 1), -chunks)
        early_info = pack(side, *[jnp.maximum(late_at + chunk, 0) for chunk in range(2)])
        late_info = pack(side, *[jnp.maximum(late_at + chunk, 0) for chunk in range(2, 4)])
        turn_info = pack((col - level) % col_count)
        solved_info = pack(side, *[(col + turn) % col_count for turn in range(col_count)])
        residual_info = pack(above, side, col ^ 3, col ^ 1, col ^ 2, col)
        place = place[None, :]
        waited = [place, start_info, rest_info, slot_info, early_info, late_info, turn_info, solved_info, residual_info, own_place]

        high, low = chain_factors(factor_info, diag_inverse, panel, per_tile, waited)
        start = start_values(start_info, shares, place, diag_inverse, chunks, width, [])

        chain_pairs = [(solver(step), solver(step + 1)) for step in range(STEPS - 1)]
        side_pairs = [(0, 0)]
        down_pairs, cross_pairs = [], []
        for c in range(col_count):
            for z in range(levels):
                for y in range(2):
                    if z > c:
                        side_pairs.append((flat(z, y, c), flat(z, y, c + 1)))
                        continue
                    cross_pairs.append((flat(z, y, c), flat(z, 1 - y, c)))
                    if z:
                        down_pairs.append((flat(z, y, c), flat(z - 1, y, c)))
        late_pairs = [(source, target) for source, target in down_pairs if source % col_count == top]
        mine, crossed = [], []

        def cross(info, arrays, waited):
            mine.append(fetch(2 * len(mine), info, store, arrays, mine[-1:] + waited))
            crossed.append(send(mine[-1], cross_pairs))

        out = pair = store = None
        start_rest = start
        last_solve = STEPS - 1 + chunks - 1
        for slot in range(last_solve + 1):
            received = [None, None, None]
            if slot:
                ups = [(flat(z, y, c), flat(z + 1, y, c)) for c in range(col_count) for z in range(c, levels - 1)
                       for y in range(2) if busy(z + c + 1, slot - 1)]
                received = [send(out, chain_pairs), send(out, side_pairs + down_pairs),
                            send(pair, ups) if ups else None]
            out, pair, store = advance(slot, slot_info, received, start, start_rest, high, low, store,
                                       [])
            if slot == 0:
                start_rest = start_values(rest_info, shares, place, diag_inverse, chunks, width, [out])

        late = [send(out, late_pairs)]
        while len(late) < chunks - 1:
            late.append(send(late[-1], late_pairs))
        pieces = solved_shares(solved_info, store, col_count)
        delivered = []
        for turn in range(1, col_count):
            pairs = [(flat(z, y, z), flat(z, y, (z + turn) % col_count)) for z in range(levels) for y in range(2)]
            delivered.append(send(pieces[turn], pairs))
        cross(early_info, [[], late[:1]], [])
        cross(late_info, [late[:2], late], [pieces[0]])
        near = [(at * col_count + here, at * col_count + (here ^ 1))
                for at in range(row_count) for here in range(col_count)]
        far = [(at * col_count + here, at * col_count + (here ^ 2))
               for at in range(row_count) for here in range(col_count)]

        size = group_rows // col_count
        parts = turned(residual_info, store, mine + crossed, series, delivered)
        def share(tile, waited):
            return residual_tiles(residual_info, tile, 1, size, padded, parts, own_place, panel, waited)

        first_give = share(0, [])
        moved_first = send(first_give, near)
        passed = added(share(2, [first_give]), moved_first)
        moved_far = send(passed, far)
        give = share(1, [passed])
        moved = send(give, near)
        own = share(3, [give, moved_far])
        solved = solved_rows(turn_info, [pieces[0]] + delivered, dates)
        residual = ((own + moved) + moved_far)[:dates]
        return solved.T, residual.T

    return body


def make_body(row_count, col_count):
    base = row_count - STEPS

    def body(series, point_order, step_block, panel, diag_inverse):
        f32 = jnp.float32
        dates, own_points = series.shape
        block = diag_inverse.shape[1]
        group_rows = panel.shape[0]
        local_blocks = group_rows // block
        per = panel.shape[1] // block
        width = -(-dates // (8 * CHUNKS)) * 8
        padded = width * CHUNKS

        def column(step):
            return step // per

        solver_col = [0] + [column(step - 1) for step in range(1, STEPS)]

        def arrival(start, distance):
            if distance >= 1:
                return start + -(-distance // 2)
            return start + 1 + (-distance) // 2

        def fits(hop):
            for step in range(STEPS):
                for earlier in range(step):
                    due = hop * step - (solver_col[step] - column(earlier))
                    if arrival(hop * earlier, step - earlier) > due:
                        return False
            return True

        hop = 1
        while not fits(hop):
            hop += 1

        def flat(row, col):
            return row * col_count + col

        def busy(start, slot):
            return 0 <= slot - start < CHUNKS

        row = lax.axis_index("rows")
        col = lax.axis_index("cols")
        step_here = row - base
        has_step = step_here >= 0
        step_safe = jnp.maximum(step_here, 0)
        solver_here = jnp.where(step_safe == 0, 0, (step_safe - 1) // per)
        is_solver = has_step & (col == solver_here)

        def send(value, pairs):
            return lax.ppermute(value, ("rows", "cols"), pairs)

        first_row = step_block[step_safe] % local_blocks * block
        inverse = lax.dynamic_slice(diag_inverse, (first_row, jnp.int32(0)), (block, block))
        factor = lax.dynamic_slice(panel, (first_row, jnp.int32(0)), (block, per * block))
        chain_factor = lax.dot_general(
            factor, inverse, (((0,), (1,)), ((), ())),
            precision=lax.Precision.HIGH, preferred_element_type=f32)

        shares = [series]
        for turn in range(1, col_count):
            pairs = [
                (flat(base + step, (solver_col[step] + turn) % col_count), flat(base + step, solver_col[step]))
                for step in range(STEPS)
            ]
            shares.append(send(series, pairs))
        gathered = jnp.concatenate(shares, axis=1)
        local_order = point_order % group_rows

        block_order = lax.dynamic_slice(local_order, (first_row,), (block,))
        place = (block_order // own_points - col) % col_count * own_points + block_order % own_points
        side = picked(gathered, place)
        start_value = lax.dot_general(
            side, inverse, (((1,), (1,)), ((), ())),
            precision=lax.Precision.HIGH, preferred_element_type=f32)
        start_value = jnp.pad(start_value, ((0, padded - dates), (0, 0))).reshape(CHUNKS, width, block)

        zero = jnp.zeros((width, block), f32)
        held = [jnp.zeros((CHUNKS + 1, width, block), f32) for _ in range(per)]
        latest = [zero] * per
        outgoing = None
        streams = [col * per + index for index in range(per)]
        gaps = [step_here - stream for stream in streams]
        starts = [hop * stream for stream in streams]

        def arrival_here(start, gap):
            return jnp.where(gap >= 1, start + (gap + 1) // 2, start + 1 + (-gap) // 2)

        arrivals = [arrival_here(start, gap) for start, gap in zip(starts, gaps)]
        due = hop * step_here - (solver_here - col)

        def pick_chunk(values, chunk):
            return lax.dynamic_index_in_dim(values, jnp.clip(chunk, 0, CHUNKS - 1), 0, keepdims=False)

        last_slot = max(arrival(hop * step, place_row - base - step)
                        for step in range(STEPS) for place_row in range(row_count)) + CHUNKS - 1
        for slot in range(last_slot + 1):
            before = slot - 1
            one_up, two_up, level, one_down, added = [], [], [], [], []
            if before >= 0:
                for step in range(STEPS):
                    source = flat(base + step, solver_col[step])
                    if busy(hop * step, before):
                        if step + 1 < STEPS:
                            one_up.append((source, flat(base + step + 1, column(step))))
                        if step + 2 < STEPS:
                            two_up.append((source, flat(base + step + 2, column(step))))
                        if solver_col[step] != column(step):
                            level.append((source, flat(base + step, column(step))))
                        if base + step >= 1:
                            one_down.append((source, flat(base + step - 1, column(step))))
                    for from_col in range(solver_col[step]):
                        if busy(hop * step - (solver_col[step] - from_col), before):
                            added.append((flat(base + step, from_col), flat(base + step, from_col + 1)))
            from_one_up = send(outgoing, one_up) if one_up else zero
            incoming = send(outgoing, added) if added else zero
            from_two_up = send(outgoing, two_up) if two_up else zero
            from_level = send(outgoing, level) if level else zero
            from_one_down = send(outgoing, one_down) if one_down else zero
            received_up, received_down = [], []
            for index in range(per):
                upward, downward = [], []
                for stream in range(index, STEPS, per):
                    for at in range(row_count):
                        gap = at - base - stream
                        if busy(arrival(hop * stream, gap), before):
                            if gap >= 1 and at + 2 < row_count:
                                upward.append((flat(at, column(stream)), flat(at + 2, column(stream))))
                            if gap <= 0 and at >= 2:
                                downward.append((flat(at, column(stream)), flat(at - 2, column(stream))))
                received_up.append(send(latest[index], upward) if upward else zero)
                received_down.append(send(latest[index], downward) if downward else zero)

            inputs = []
            for index in range(per):
                gap = gaps[index]
                up = jnp.where(gap == 1, from_one_up, jnp.where(gap == 2, from_two_up, received_up[index]))
                same = jnp.where(col == solver_here, zero if outgoing is None else outgoing, from_level)
                down = jnp.where(gap == 0, same, jnp.where(gap == -1, from_one_down, received_down[index]))
                got = jnp.where(gap >= 1, up, down)
                chunk = slot - arrivals[index]
                valid = (chunk >= 0) & (chunk < CHUNKS)
                needed = slot - due
                ready = jnp.where(needed == chunk, up, pick_chunk(held[index], needed))
                inputs.append(jnp.where((gap >= 1) & has_step, ready, 0))
                held[index] = lax.dynamic_update_index_in_dim(
                    held[index], got, jnp.where(valid, chunk, CHUNKS), 0)
                latest[index] = got
            if slot <= hop * (STEPS - 1) + CHUNKS - 1:
                total = incoming + jnp.dot(
                    jnp.concatenate(inputs, axis=1), chain_factor,
                    precision=lax.Precision.HIGH, preferred_element_type=f32)
                outgoing = jnp.where(is_solver, pick_chunk(start_value, slot - due) - total, total)

        whole = [values[:CHUNKS].reshape(padded, block)[:dates] for values in held]
        out_rows = STEPS * block // (row_count * col_count)

        def wanted(at):
            return at * col_count * out_rows // block

        source_col = row * col_count * out_rows // block // per
        stream_index = row * col_count * out_rows // block % per
        chosen = whole[0]
        for index in range(1, per):
            chosen = jnp.where(stream_index == index, whole[index], chosen)

        def piece(target):
            first = (row * col_count + target) * out_rows % block
            return lax.dynamic_slice(chosen, (jnp.int32(0), first), (dates, out_rows))

        solved = piece(col)
        for turn in range(1, col_count):
            pairs = [
                (flat(at, column(wanted(at))), flat(at, (column(wanted(at)) + turn) % col_count))
                for at in range(row_count)
            ]
            moved = send(piece((col + turn) % col_count), pairs)
            solved = jnp.where((col - source_col) % col_count == turn, moved, solved)

        away = local_order // own_points != col
        own_place = jnp.where(away, -1, local_order % own_points)
        product = lax.dot_general(
            jnp.concatenate(whole, axis=1), panel, (((1,), (1,)), ((), ())),
            precision=lax.Precision.HIGH, preferred_element_type=f32)
        left = picked(series, own_place) - product
        distance = 1
        parts = left.reshape(dates, col_count, group_rows // col_count)
        pieces = [parts[:, index] for index in range(col_count)]
        while distance < col_count:
            bit = (col // distance) % 2
            keep, give = [], []
            for index in range(0, len(pieces), 2):
                keep.append(jnp.where(bit == 0, pieces[index], pieces[index + 1]))
                give.append(jnp.where(bit == 0, pieces[index + 1], pieces[index]))
            pairs = [(flat(at, here), flat(at, here ^ distance)) for at in range(row_count) for here in range(col_count)]
            moved = send(jnp.concatenate(give, axis=1) if len(give) > 1 else give[0], pairs)
            size = group_rows // col_count
            pieces = [value + moved[:, index * size:(index + 1) * size] for index, value in enumerate(keep)]
            distance *= 2
        return solved.T, pieces[0].T

    return body


def solution(mesh):
    in_specs = (P(None, ("rows", "cols")), P("rows"), P(), P("rows", "cols"), P("rows", None))
    out_specs = (P(("rows", "cols"), None), P(("rows", "cols"), None))
    row_count, col_count = mesh.shape["rows"], mesh.shape["cols"]
    lines = row_count == STEPS and 2 * col_count == STEPS
    body = (make_line_body if lines else make_body)(row_count, col_count)
    return jax.shard_map(body, mesh=mesh, in_specs=in_specs, out_specs=out_specs, check_vma=False)
```

```python
import jax
import jax.numpy as jnp
from jax import lax
from jax.experimental import pallas as pl
from jax.experimental.pallas import tpu as pltpu
from jax.sharding import PartitionSpec as P

STEPS = 8
CHUNKS = 4
LINE_CHUNKS = 4
TILE = 512


def split_hi(value):
    return lax.reduce_precision(value, 8, 7)


def halves(value):
    high = value.astype(jnp.bfloat16)
    return high, (value - high.astype(jnp.float32)).astype(jnp.bfloat16)


def one_hot(index, depth):
    return (lax.broadcasted_iota(jnp.int32, (depth, index.shape[0]), 0) == index[None, :]).astype(jnp.bfloat16)


def picked(values, index):
    chosen = one_hot(index, values.shape[1])
    high = split_hi(values)
    low = split_hi(values - high)
    return (jnp.dot(high.astype(jnp.bfloat16), chosen, preferred_element_type=jnp.float32)
            + jnp.dot(low.astype(jnp.bfloat16), chosen, preferred_element_type=jnp.float32))


def dot_nt(left, right):
    return lax.dot_general(left, right, (((1,), (1,)), ((), ())), preferred_element_type=jnp.float32)


def in_vmem(value):
    return pltpu.with_memory_space_constraint(value, pltpu.VMEM)


def in_hbm(value):
    return pltpu.with_memory_space_constraint(value, pltpu.HBM)


def vmem_shape(shape, dtype):
    return pltpu.VMEM(shape, dtype)


def hbm_shape(shape, dtype):
    return pltpu.HBM(shape, dtype)


def factor_kernel(info, inverse_ref, panel_ref, *rest):
    high_ref, low_ref, inverse_high, inverse_low = rest[-4:]
    tile = pl.program_id(0)

    @pl.when(tile == 0)
    def _():
        high, low = halves(inverse_ref[...])
        inverse_high[...] = high
        inverse_low[...] = low

    @pl.when(tile <= info[1])
    def _():
        high, low = halves(panel_ref[...])
        value = (jnp.dot(inverse_high[...], high, preferred_element_type=jnp.float32)
                 + jnp.dot(inverse_low[...], high, preferred_element_type=jnp.float32)
                 + jnp.dot(inverse_high[...], low, preferred_element_type=jnp.float32))
        high, low = halves(value.T)
        high_ref[...] = high
        low_ref[...] = low


def chain_factors(info, diag_inverse, panel, tile, waited):
    block = diag_inverse.shape[1]
    depth = panel.shape[1]
    shape = vmem_shape((depth, block), jnp.bfloat16)
    return pl.pallas_call(
        factor_kernel,
        out_shape=[shape, shape],
        grid_spec=pltpu.PrefetchScalarGridSpec(
            num_scalar_prefetch=1,
            grid=(depth // tile,),
            in_specs=[
                pl.BlockSpec((block, block), lambda t, info: (info[0], 0)),
                pl.BlockSpec((block, tile), lambda t, info: (info[0], jnp.minimum(t, info[1]))),
            ] + [pl.BlockSpec(memory_space=pl.ANY)] * len(waited),
            out_specs=[pl.BlockSpec((tile, block), lambda t, info: (jnp.minimum(t, info[1]), 0))] * 2,
            scratch_shapes=[pltpu.VMEM((block, block), jnp.bfloat16)] * 2,
        ),
        compiler_params=pltpu.CompilerParams(vmem_limit_bytes=44 << 20),
        cost_estimate=pl.CostEstimate(
            flops=6 * block * block * depth, bytes_accessed=4 * block * (block + 2 * depth), transcendentals=0),
    )(info, in_hbm(diag_inverse), in_hbm(panel), *waited)


def start_kernel(info, *refs):
    shares, (place_ref, source_ref), (out_ref, inverse_ref, side, high, low, sem) = refs[:-8], refs[-8:-6], refs[-6:]
    dates, points = shares[0].shape
    lanes = high.shape[1]
    chunks, width, block = out_ref.shape
    tile = 256
    steps = block // tile

    @pl.when(info[1] == 1)
    def _():
        def inverse_rows(step):
            rows = pl.ds(pl.multiple_of(step * tile, tile), tile)
            source = pl.ds(pl.multiple_of(info[0] * block + step * tile, tile), tile)
            return pltpu.make_async_copy(source_ref.at[source], inverse_ref.at[rows], sem.at[step])

        for step in range(steps):
            inverse_rows(step).start()
        side[...] = jnp.zeros_like(side)
        for index, share in enumerate(shares):
            columns = pl.ds(index * points, points)
            first, second = halves(share[...])
            side[pl.ds(0, dates), columns] = first
            side[pl.ds(lanes, dates), columns] = second

        def order(step, carry):
            columns = pl.ds(pl.multiple_of(step * tile, tile), tile)
            places = lax.broadcasted_iota(jnp.int32, (side.shape[1], tile), 0)
            chosen = jnp.where(places == place_ref[:, columns], 1.0, 0.0).astype(jnp.bfloat16)
            both = jnp.dot(side[...], chosen, preferred_element_type=jnp.float32)
            first, second = halves((both[:lanes] + both[lanes:]).T)
            high[columns] = first
            low[columns] = second
            return carry

        def multiply(step, carry):
            rows = pl.ds(pl.multiple_of(step * tile, tile), tile)
            inverse_rows(step).wait()
            first, second = halves(inverse_ref[rows])
            value = (jnp.dot(first, high[...], preferred_element_type=jnp.float32)
                     + jnp.dot(second, high[...], preferred_element_type=jnp.float32)
                     + jnp.dot(first, low[...], preferred_element_type=jnp.float32)).T
            for chunk in range(chunks):
                out_ref[chunk, :, rows] = value[chunk * width:(chunk + 1) * width]
            return carry

        lax.fori_loop(0, steps, order, 0)
        lax.fori_loop(0, steps, multiply, 0)


def start_values(info, shares, place, diag_inverse, chunks, width, waited):
    block = diag_inverse.shape[1]
    dates, points = shares[0].shape
    lanes = -(-max(dates, chunks * width) // 128) * 128
    count = len(shares) + 2
    ordered = pltpu.VMEM((block, lanes), jnp.bfloat16)

    def kernel(info, *refs):
        start_kernel(info, *refs[:count], *refs[-6:])

    whole = pl.BlockSpec(memory_space=pltpu.VMEM)
    return pl.pallas_call(
        kernel,
        out_shape=vmem_shape((chunks, width, block), jnp.float32),
        in_specs=[pl.BlockSpec(memory_space=pltpu.SMEM)] + [whole] * (count - 1)
        + [pl.BlockSpec(memory_space=pl.ANY)] * (1 + len(waited)),
        out_specs=whole,
        scratch_shapes=[
            pltpu.VMEM((block, block), jnp.float32),
            pltpu.VMEM((2 * lanes, len(shares) * points), jnp.bfloat16),
            ordered,
            ordered,
            pltpu.SemaphoreType.DMA((block // 256,)),
        ],
        compiler_params=pltpu.CompilerParams(vmem_limit_bytes=28 << 20),
        cost_estimate=pl.CostEstimate(
            flops=10 * dates * block * block, bytes_accessed=4 * block * (block + 2 * dates), transcendentals=0),
    )(info, *map(in_vmem, shares), in_vmem(place), in_hbm(diag_inverse), *waited)


def slot_kernel(slot, chunks, sent, info, *refs):
    refs = list(refs)
    chain_ref = refs.pop(0) if sent[0] else None
    side_ref = refs.pop(0) if sent[1] else None
    up_ref = refs.pop(0) if sent[2] else None
    start_ref, start_rest_ref, high_ref, low_ref, out_ref, pair_ref, store_ref, sem = refs
    width, block = out_ref.shape
    first, second = pair_ref.at[pl.ds(0, width)], pair_ref.at[pl.ds(width, width)]
    chunk = slot - info[8]
    stored = (chunk >= 0) & (chunk < chunks)

    def keep_pair(action):
        @pl.when(stored & (info[1] == 2))
        def _():
            for stream in range(2):
                action(pltpu.make_async_copy(
                    pair_ref.at[pl.ds(stream * width, width)], store_ref.at[chunk, stream], sem.at[stream]))

    def keep_line(action):
        @pl.when(stored & (info[1] != 2))
        def _():
            action(pltpu.make_async_copy(out_ref, store_ref.at[chunk, info[9]], sem.at[0]))

    @pl.when(info[0] == 1)
    def _():
        out_ref[...] = side_ref[...] if sent[1] else jnp.zeros_like(out_ref)

    @pl.when(info[0] == 0)
    def _():
        out_ref[...] = jnp.zeros_like(out_ref)

    for code, ref in enumerate((side_ref, chain_ref, None if up_ref is None else up_ref.at[pl.ds(0, width)])):
        if ref is not None:
            @pl.when(info[1] == code)
            def _(ref=ref):
                first[...] = ref[...]
    for code, ref in enumerate((None if up_ref is None else up_ref.at[pl.ds(width, width)], chain_ref)):
        if ref is not None:
            @pl.when(info[2] == code)
            def _(ref=ref):
                second[...] = ref[...]

    keep_pair(lambda copy: copy.start())

    if any(sent):
        def step(tile, carry):
            per_stream = block // TILE
            rows = pl.ds(pl.multiple_of(tile // per_stream * width, 16), width)
            columns = pl.ds(pl.multiple_of(tile % per_stream * TILE, TILE), TILE)
            factor = pl.ds(pl.multiple_of(tile * TILE, TILE), TILE)
            high, low = halves(pair_ref[rows, columns])
            both = jnp.dot(jnp.concatenate([high, low], axis=0), high_ref[factor], preferred_element_type=jnp.float32)
            rest = jnp.dot(high, low_ref[factor], preferred_element_type=jnp.float32)
            out_ref[...] += (both[:width] + both[width:]) + rest
            return carry

        lax.fori_loop(0, info[3], step, 0)

    at = jnp.clip(slot - info[6], 0, chunks - 1)
    for code, ref in enumerate((start_ref, start_rest_ref)):
        @pl.when((info[4] == 1) & (info[10] == code))
        def _(ref=ref):
            out_ref[...] = ref[at] - out_ref[...]

    @pl.when(info[5] == 1)
    def _():
        second[...] = out_ref[...]

    if sent[1]:
        @pl.when(info[7] == 1)
        def _():
            out_ref[...] = side_ref[...]

    keep_line(lambda copy: copy.start())
    keep_line(lambda copy: copy.wait())
    keep_pair(lambda copy: copy.wait())


def advance(slot, info, received, start, start_rest, high, low, store, waited):
    chunks, width, block = start.shape
    sent = tuple(value is not None for value in received)
    operands = [in_vmem(value) for value in received if value is not None]
    operands += [in_vmem(start), in_vmem(start_rest), in_vmem(high), in_vmem(low)]
    count = len(operands)
    extra = list(waited) + ([] if store is None else [in_hbm(store)])

    def kernel(info, *refs):
        slot_kernel(slot, chunks, sent, info, *refs[:count], *refs[-4:])

    return pl.pallas_call(
        kernel,
        out_shape=[vmem_shape((width, block), jnp.float32), vmem_shape((2 * width, block), jnp.float32),
                   hbm_shape((chunks, 2, width, block), jnp.float32)],
        in_specs=[pl.BlockSpec(memory_space=pltpu.SMEM)] + [pl.BlockSpec(memory_space=pltpu.VMEM)] * count
        + [pl.BlockSpec(memory_space=pl.ANY)] * len(extra),
        out_specs=[pl.BlockSpec(memory_space=pltpu.VMEM)] * 2 + [pl.BlockSpec(memory_space=pl.ANY)],
        scratch_shapes=[pltpu.SemaphoreType.DMA((2,))],
        input_output_aliases={} if store is None else {count + len(extra): 2},
        compiler_params=pltpu.CompilerParams(vmem_limit_bytes=16 << 20),
        cost_estimate=pl.CostEstimate(
            flops=6 * width * block * high.shape[0], bytes_accessed=32 * width * block, transcendentals=0),
    )(info, *operands, *extra)


def fetch(first_chunk, info, store, arrays, waited):
    _, _, width, block = store.shape
    counts = [len(group) for group in arrays]
    flat_arrays = [array for group in arrays for array in group]

    def kernel(info, store_ref, *refs):
        out_ref, sem = refs[-2:]

        def copies(action):
            for index in range(len(arrays)):
                @pl.when(info[1 + index] == 0)
                def _(index=index):
                    action(pltpu.make_async_copy(store_ref.at[first_chunk + index, info[0]],
                                                 out_ref.at[pl.ds(index * width, width)], sem.at[index]))

        copies(lambda copy: copy.start())
        left = list(refs[:len(flat_arrays)])
        for index, count in enumerate(counts):
            for place in range(count):
                ref = left.pop(0)

                @pl.when(info[1 + index] == place + 1)
                def _(index=index, ref=ref):
                    out_ref[pl.ds(index * width, width)] = ref[...]
        copies(lambda copy: copy.wait())

    return pl.pallas_call(
        kernel,
        out_shape=vmem_shape((len(arrays) * width, block), jnp.float32),
        in_specs=[pl.BlockSpec(memory_space=pltpu.SMEM), pl.BlockSpec(memory_space=pl.ANY)]
        + [pl.BlockSpec(memory_space=pltpu.VMEM)] * len(flat_arrays) + [pl.BlockSpec(memory_space=pl.ANY)] * len(waited),
        out_specs=pl.BlockSpec(memory_space=pltpu.VMEM),
        scratch_shapes=[pltpu.SemaphoreType.DMA((len(arrays),))],
        compiler_params=pltpu.CompilerParams(vmem_limit_bytes=16 << 20),
        cost_estimate=pl.CostEstimate(flops=0, bytes_accessed=0, transcendentals=0),
    )(info, in_hbm(store), *map(in_vmem, flat_arrays), *waited)


def solved_shares(info, store, shares):
    chunks, _, width, block = store.shape
    size = block // shares

    def kernel(info, store_ref, *refs):
        outs, sem = refs[:-1], refs[-1]

        def copies(action):
            for chunk in range(chunks):
                for turn in range(shares):
                    columns = pl.ds(pl.multiple_of(info[1 + turn] * size, size), size)
                    action(pltpu.make_async_copy(store_ref.at[chunk, info[0], :, columns],
                                                 outs[turn].at[pl.ds(chunk * width, width)], sem.at[chunk, turn]))

        copies(lambda copy: copy.start())
        copies(lambda copy: copy.wait())

    return pl.pallas_call(
        kernel,
        out_shape=[vmem_shape((chunks * width, size), jnp.float32)] * shares,
        in_specs=[pl.BlockSpec(memory_space=pltpu.SMEM), pl.BlockSpec(memory_space=pl.ANY)],
        out_specs=[pl.BlockSpec(memory_space=pltpu.VMEM)] * shares,
        scratch_shapes=[pltpu.SemaphoreType.DMA((chunks, shares))],
        compiler_params=pltpu.CompilerParams(vmem_limit_bytes=16 << 20),
        cost_estimate=pl.CostEstimate(flops=0, bytes_accessed=0, transcendentals=0),
    )(info, in_hbm(store))


def turn_kernel(info, chunks, width, store_ref, *refs):
    pairs = chunks // 2
    lines, crossed, series_ref = refs[:pairs], refs[pairs:2 * pairs], refs[2 * pairs]
    both, side_high, side_low, raw, side, sem = refs[-6:]
    block = raw.shape[2]
    dates = series_ref.shape[0]
    total = chunks * width

    def copies(action):
        for chunk in range(chunks):
            rows = pl.ds(chunk * width, width)

            @pl.when(info[0] == 1)
            def _(chunk=chunk, rows=rows):
                for stream in range(2):
                    action(pltpu.make_async_copy(
                        store_ref.at[chunk, stream], raw.at[stream, rows], sem.at[2 * chunk + stream]))

        for pair in range(pairs):
            rows = pl.ds(2 * pair * width, 2 * width)

            @pl.when(info[0] == 0)
            def _(pair=pair, rows=rows):
                action(pltpu.make_async_copy(lines[pair], raw.at[info[1], rows], sem.at[2 * pair]))
                action(pltpu.make_async_copy(crossed[pair], raw.at[1 - info[1], rows], sem.at[2 * pair + 1]))

    copies(lambda copy: copy.start())
    lanes = side.shape[0]
    side[...] = jnp.zeros_like(side)
    side[pl.ds(0, dates)] = series_ref[...]
    first, second = halves(side[...].T)
    side_high[...] = first
    side_low[...] = second
    raw[:, pl.ds(total, lanes - total)] = jnp.zeros((2, lanes - total, block), jnp.float32)
    copies(lambda copy: copy.wait())
    for stream in range(2):
        first, second = halves(raw[stream].T)
        both[pl.ds(stream * block, block), pl.ds(0, lanes)] = first
        both[pl.ds(stream * block, block), pl.ds(lanes, lanes)] = second


def turned(info, store, sources, series, waited):
    chunks, _, width, block = store.shape
    dates, points = series.shape
    lanes = -(-max(dates, chunks * width) // 128) * 128
    count = 2 + len(sources)

    def kernel(info, *refs):
        turn_kernel(info, chunks, width, *refs[:count], *refs[count + len(waited):])

    whole = pl.BlockSpec(memory_space=pltpu.VMEM)
    solved = vmem_shape((2 * block, 2 * lanes), jnp.bfloat16)
    side = vmem_shape((points, lanes), jnp.bfloat16)
    return pl.pallas_call(
        kernel,
        out_shape=[solved, side, side],
        in_specs=[pl.BlockSpec(memory_space=pltpu.SMEM)] + [pl.BlockSpec(memory_space=pl.ANY)] * (1 + len(sources))
        + [whole] + [pl.BlockSpec(memory_space=pl.ANY)] * len(waited),
        out_specs=[whole] * 3,
        scratch_shapes=[
            pltpu.VMEM((2, lanes, block), jnp.float32),
            pltpu.VMEM((lanes, points), jnp.float32),
            pltpu.SemaphoreType.DMA((2 * chunks,)),
        ],
        compiler_params=pltpu.CompilerParams(vmem_limit_bytes=16 << 20),
        cost_estimate=pl.CostEstimate(flops=0, bytes_accessed=0, transcendentals=0),
    )(info, in_hbm(store), *sources, in_vmem(series), *waited)


def residual_kernel(info, first_tile, tiles, both, side_high, side_low, place_ref, panel_ref, *rest):
    out_ref, held, sem = rest[-3:]
    steps, rows = held.shape[:2]
    total = out_ref.shape[0]
    per_tile = steps // tiles

    def source_rows(step):
        start = info[2 + first_tile + step // per_tile] * (per_tile * rows) + step % per_tile * rows
        return pl.ds(pl.multiple_of(start, rows), rows)

    def panel_rows(step):
        return pltpu.make_async_copy(panel_ref.at[source_rows(step)], held.at[step], sem.at[step])

    for step in range(steps):
        panel_rows(step).start()

    def multiply(step, carry):
        panel_rows(step).wait()
        factor_high, factor_low = halves(held[step])
        lanes = side_high.shape[1]
        wide = jnp.dot(factor_high, both[...], preferred_element_type=jnp.float32)
        product = ((wide[:, :lanes] + wide[:, lanes:])
                   + jnp.dot(factor_low, both[:, pl.ds(0, lanes)], preferred_element_type=jnp.float32))
        places = lax.broadcasted_iota(jnp.int32, (rows, side_high.shape[0]), 1)
        chosen = jnp.where(places == place_ref[source_rows(step)], 1.0, 0.0).astype(jnp.bfloat16)
        value = (jnp.dot(chosen, side_high[...], preferred_element_type=jnp.float32)
                 + jnp.dot(chosen, side_low[...], preferred_element_type=jnp.float32)) - product
        out_ref[:, pl.ds(pl.multiple_of(step * rows, rows), rows)] = value.T[:total]
        return carry

    lax.fori_loop(0, steps, multiply, 0)


def residual_tiles(info, first_tile, tiles, size, total, parts, place, panel, waited):
    depth = panel.shape[1]
    rows = 256
    steps = tiles * size // rows

    def kernel(info, *refs):
        residual_kernel(info, first_tile, tiles, *refs[:5], *refs[-3:])

    whole = pl.BlockSpec(memory_space=pltpu.VMEM)
    return pl.pallas_call(
        kernel,
        out_shape=vmem_shape((total, tiles * size), jnp.float32),
        in_specs=[pl.BlockSpec(memory_space=pltpu.SMEM)] + [whole] * 4
        + [pl.BlockSpec(memory_space=pl.ANY)] * (1 + len(waited)),
        out_specs=whole,
        scratch_shapes=[pltpu.VMEM((steps, rows, depth), jnp.float32), pltpu.SemaphoreType.DMA((steps,))],
        compiler_params=pltpu.CompilerParams(vmem_limit_bytes=36 << 20),
        cost_estimate=pl.CostEstimate(
            flops=6 * total * tiles * size * depth, bytes_accessed=4 * tiles * size * depth, transcendentals=0),
    )(info, *map(in_vmem, parts), in_vmem(place), in_hbm(panel), *waited)


def solved_rows(info, shares, dates):
    def kernel(info, *refs):
        for index, ref in enumerate(refs[:-1]):
            @pl.when(info[0] == index)
            def _(ref=ref):
                refs[-1][...] = ref[pl.ds(0, dates)]

    whole = pl.BlockSpec(memory_space=pltpu.VMEM)
    return pl.pallas_call(
        kernel,
        out_shape=jax.ShapeDtypeStruct((dates, shares[0].shape[1]), jnp.float32),
        in_specs=[pl.BlockSpec(memory_space=pltpu.SMEM)] + [whole] * len(shares),
        out_specs=whole,
        compiler_params=pltpu.CompilerParams(vmem_limit_bytes=16 << 20),
    )(info, *map(in_vmem, shares))


def add_kernel(left_ref, right_ref, out_ref):
    out_ref[...] = left_ref[...] + right_ref[:, pl.ds(0, out_ref.shape[1])]


def added(left, right):
    whole = pl.BlockSpec(memory_space=pltpu.VMEM)
    return pl.pallas_call(
        add_kernel,
        out_shape=vmem_shape(left.shape, left.dtype),
        in_specs=[whole] * 2,
        out_specs=whole,
        compiler_params=pltpu.CompilerParams(vmem_limit_bytes=16 << 20),
    )(in_vmem(left), in_vmem(right))


def make_line_body(row_count, col_count):
    levels = row_count // 2
    chunks = LINE_CHUNKS

    def flat(level, side, col):
        return (2 * level + side) * col_count + col

    def body(series, point_order, step_block, panel, diag_inverse):
        f32 = jnp.float32
        dates, own_points = series.shape
        block = diag_inverse.shape[1]
        group_rows, depth = panel.shape
        local_blocks = group_rows // block
        width = -(-dates // (16 * chunks)) * 16
        padded = width * chunks
        row = lax.axis_index("rows")
        col = lax.axis_index("cols")
        level, side = row // 2, row % 2

        def send(value, pairs):
            return lax.ppermute(value, ("rows", "cols"), pairs)

        def solver(step):
            return flat(step // 2, step % 2, max(step - 1, 0) // 2)

        def busy(start, slot):
            return 0 <= slot - start < chunks

        above, same = level > col, level == col
        second_solver = same & (side == 1)
        last = (side == 0) & (level == col + 1)
        origin = (row == 0) & (col == 0)
        is_solver = second_solver | last | origin

        shares = [series]
        for turn in range(1, col_count):
            pairs = []
            for step in range(STEPS):
                here = max(step - 1, 0) // 2
                pairs.append((flat(step // 2, step % 2, (here + turn) % col_count), flat(step // 2, step % 2, here)))
            shares.append(send(series, pairs))

        per_tile = 256
        top = levels - 1
        last_factor = jnp.where(above, depth // per_tile - 1, jnp.where(second_solver, block // per_tile - 1, 0))
        slot_index = step_block[row] % local_blocks
        local_order = point_order % group_rows
        block_order = lax.dynamic_slice(local_order, (slot_index * block,), (block,))
        place = (block_order // own_points - col) % col_count * own_points + block_order % own_points
        first_direct = 2 * top + 2
        arrived = jnp.where(origin, 0, jnp.where((col == top) & (level == top - 1), first_direct, 3 * col - level + 1))
        from_direct = (col == top) & (level < top - 1)
        stored_at = jnp.where(above, level + col + 1, jnp.where(from_direct, first_direct + 4 * chunks, arrived))
        own_place = jnp.where(local_order // own_points != col, -1, local_order % own_points)[:, None]
        def pack(*values):
            return jnp.stack([jnp.asarray(value).astype(jnp.int32) for value in values])

        factor_info = pack(slot_index, last_factor)
        start_info = pack(slot_index, origin)
        rest_info = pack(slot_index, is_solver & jnp.logical_not(origin))
        slot_info = pack(
            (above | second_solver) & (col > 0),
            jnp.where(above, 2, jnp.where(second_solver, 1, 0)),
            last,
            jnp.where(above, depth // TILE, jnp.where(second_solver, block // TILE, 0)),
            is_solver,
            second_solver,
            jnp.where(origin, 0, level + col + 1),
            jnp.logical_not(above | second_solver | origin),
            stored_at,
            side,
            jnp.logical_not(origin),
        )
        usual = jnp.where(from_direct, level + 1, 0)
        fetch_info = pack(side, usual, usual)
        turn_info = pack((col - level) % col_count)
        late_info = pack(side, usual, jnp.where((col == top) & (level == top - 1), top, usual))
        solved_info = pack(side, *[(col + turn) % col_count for turn in range(col_count)])
        residual_info = pack(above, side, col ^ 3, col ^ 1, col ^ 2, col)
        place = place[None, :]
        waited = [place, start_info, rest_info, slot_info, fetch_info, late_info, turn_info, solved_info, residual_info, own_place]

        high, low = chain_factors(factor_info, diag_inverse, panel, per_tile, waited)
        start = start_values(start_info, shares, place, diag_inverse, chunks, width, [])

        chain_pairs = [(solver(step), solver(step + 1)) for step in range(STEPS - 1)]
        side_pairs = [(0, 0)]
        down_pairs, cross_pairs = [], []
        for c in range(col_count):
            for z in range(levels):
                for y in range(2):
                    if z > c:
                        side_pairs.append((flat(z, y, c), flat(z, y, c + 1)))
                        continue
                    cross_pairs.append((flat(z, y, c), flat(z, 1 - y, c)))
                    if z and (c < levels - 1 or z == c):
                        down_pairs.append((flat(z, y, c), flat(z - 1, y, c)))
        direct_pairs = [[(flat(top, y, top), flat(z, y, top)) for y in range(2)] for z in range(top)]
        late_pairs = direct_pairs[top - 1]
        mine, crossed, direct = [], [], []

        def send_direct():
            direct.append([send(out, direct_pairs[z]) for z in range(top - 1)])

        def cross(info, arrays, waited):
            mine.append(fetch(2 * len(mine), info, store, arrays, mine[-1:] + waited))
            crossed.append(send(mine[-1], cross_pairs))

        out = pair = store = None
        start_rest = start
        last_solve = STEPS - 1 + chunks - 1
        for slot in range(last_solve + 1):
            received = [None, None, None]
            if slot:
                ups = [(flat(z, y, c), flat(z + 1, y, c)) for c in range(col_count) for z in range(c, levels - 1)
                       for y in range(2) if busy(z + c + 1, slot - 1)]
                received = [send(out, chain_pairs), send(out, side_pairs + down_pairs),
                            send(pair, ups) if ups else None]
            if slot >= first_direct:
                send_direct()
            out, pair, store = advance(slot, slot_info, received, start, start_rest, high, low, store,
                                       mine[-1:] + (direct[-2] if len(direct) > 1 else []))
            if slot == 0:
                start_rest = start_values(rest_info, shares, place, diag_inverse, chunks, width, [out])
            if slot == first_direct + 1:
                cross(fetch_info, direct, [])

        send_direct()
        late = send(out, late_pairs)
        pieces = solved_shares(solved_info, store, col_count)
        delivered = []
        for turn in range(1, col_count):
            pairs = [(flat(z, y, z), flat(z, y, (z + turn) % col_count)) for z in range(levels) for y in range(2)]
            delivered.append(send(pieces[turn], pairs))
        cross(late_info, [direct[-2], direct[-1] + [late]], [pieces[0]])
        near = [(at * col_count + here, at * col_count + (here ^ 1))
                for at in range(row_count) for here in range(col_count)]
        far = [(at * col_count + here, at * col_count + (here ^ 2))
               for at in range(row_count) for here in range(col_count)]

        size = group_rows // col_count
        parts = turned(residual_info, store, mine + crossed, series, delivered)
        def share(tile, waited):
            return residual_tiles(residual_info, tile, 1, size, padded, parts, own_place, panel, waited)

        first_give = share(0, [])
        moved_first = send(first_give, near)
        passed = added(share(2, [first_give]), moved_first)
        moved_far = send(passed, far)
        give = share(1, [passed])
        moved = send(give, near)
        own = share(3, [give, moved_far])
        solved = solved_rows(turn_info, [pieces[0]] + delivered, dates)
        residual = ((own + moved) + moved_far)[:dates]
        return solved.T, residual.T

    return body


def make_body(row_count, col_count):
    base = row_count - STEPS

    def body(series, point_order, step_block, panel, diag_inverse):
        f32 = jnp.float32
        dates, own_points = series.shape
        block = diag_inverse.shape[1]
        group_rows = panel.shape[0]
        local_blocks = group_rows // block
        per = panel.shape[1] // block
        width = -(-dates // (8 * CHUNKS)) * 8
        padded = width * CHUNKS

        def column(step):
            return step // per

        solver_col = [0] + [column(step - 1) for step in range(1, STEPS)]

        def arrival(start, distance):
            if distance >= 1:
                return start + -(-distance // 2)
            return start + 1 + (-distance) // 2

        def fits(hop):
            for step in range(STEPS):
                for earlier in range(step):
                    due = hop * step - (solver_col[step] - column(earlier))
                    if arrival(hop * earlier, step - earlier) > due:
                        return False
            return True

        hop = 1
        while not fits(hop):
            hop += 1

        def flat(row, col):
            return row * col_count + col

        def busy(start, slot):
            return 0 <= slot - start < CHUNKS

        row = lax.axis_index("rows")
        col = lax.axis_index("cols")
        step_here = row - base
        has_step = step_here >= 0
        step_safe = jnp.maximum(step_here, 0)
        solver_here = jnp.where(step_safe == 0, 0, (step_safe - 1) // per)
        is_solver = has_step & (col == solver_here)

        def send(value, pairs):
            return lax.ppermute(value, ("rows", "cols"), pairs)

        first_row = step_block[step_safe] % local_blocks * block
        inverse = lax.dynamic_slice(diag_inverse, (first_row, jnp.int32(0)), (block, block))
        factor = lax.dynamic_slice(panel, (first_row, jnp.int32(0)), (block, per * block))
        chain_factor = lax.dot_general(
            factor, inverse, (((0,), (1,)), ((), ())),
            precision=lax.Precision.HIGH, preferred_element_type=f32)

        shares = [series]
        for turn in range(1, col_count):
            pairs = [
                (flat(base + step, (solver_col[step] + turn) % col_count), flat(base + step, solver_col[step]))
                for step in range(STEPS)
            ]
            shares.append(send(series, pairs))
        gathered = jnp.concatenate(shares, axis=1)
        local_order = point_order % group_rows

        block_order = lax.dynamic_slice(local_order, (first_row,), (block,))
        place = (block_order // own_points - col) % col_count * own_points + block_order % own_points
        side = picked(gathered, place)
        start_value = lax.dot_general(
            side, inverse, (((1,), (1,)), ((), ())),
            precision=lax.Precision.HIGH, preferred_element_type=f32)
        start_value = jnp.pad(start_value, ((0, padded - dates), (0, 0))).reshape(CHUNKS, width, block)

        zero = jnp.zeros((width, block), f32)
        held = [jnp.zeros((CHUNKS + 1, width, block), f32) for _ in range(per)]
        latest = [zero] * per
        outgoing = None
        streams = [col * per + index for index in range(per)]
        gaps = [step_here - stream for stream in streams]
        starts = [hop * stream for stream in streams]

        def arrival_here(start, gap):
            return jnp.where(gap >= 1, start + (gap + 1) // 2, start + 1 + (-gap) // 2)

        arrivals = [arrival_here(start, gap) for start, gap in zip(starts, gaps)]
        due = hop * step_here - (solver_here - col)

        def pick_chunk(values, chunk):
            return lax.dynamic_index_in_dim(values, jnp.clip(chunk, 0, CHUNKS - 1), 0, keepdims=False)

        last_slot = max(arrival(hop * step, place_row - base - step)
                        for step in range(STEPS) for place_row in range(row_count)) + CHUNKS - 1
        for slot in range(last_slot + 1):
            before = slot - 1
            one_up, two_up, level, one_down, added = [], [], [], [], []
            if before >= 0:
                for step in range(STEPS):
                    source = flat(base + step, solver_col[step])
                    if busy(hop * step, before):
                        if step + 1 < STEPS:
                            one_up.append((source, flat(base + step + 1, column(step))))
                        if step + 2 < STEPS:
                            two_up.append((source, flat(base + step + 2, column(step))))
                        if solver_col[step] != column(step):
                            level.append((source, flat(base + step, column(step))))
                        if base + step >= 1:
                            one_down.append((source, flat(base + step - 1, column(step))))
                    for from_col in range(solver_col[step]):
                        if busy(hop * step - (solver_col[step] - from_col), before):
                            added.append((flat(base + step, from_col), flat(base + step, from_col + 1)))
            from_one_up = send(outgoing, one_up) if one_up else zero
            incoming = send(outgoing, added) if added else zero
            from_two_up = send(outgoing, two_up) if two_up else zero
            from_level = send(outgoing, level) if level else zero
            from_one_down = send(outgoing, one_down) if one_down else zero
            received_up, received_down = [], []
            for index in range(per):
                upward, downward = [], []
                for stream in range(index, STEPS, per):
                    for at in range(row_count):
                        gap = at - base - stream
                        if busy(arrival(hop * stream, gap), before):
                            if gap >= 1 and at + 2 < row_count:
                                upward.append((flat(at, column(stream)), flat(at + 2, column(stream))))
                            if gap <= 0 and at >= 2:
                                downward.append((flat(at, column(stream)), flat(at - 2, column(stream))))
                received_up.append(send(latest[index], upward) if upward else zero)
                received_down.append(send(latest[index], downward) if downward else zero)

            inputs = []
            for index in range(per):
                gap = gaps[index]
                up = jnp.where(gap == 1, from_one_up, jnp.where(gap == 2, from_two_up, received_up[index]))
                same = jnp.where(col == solver_here, zero if outgoing is None else outgoing, from_level)
                down = jnp.where(gap == 0, same, jnp.where(gap == -1, from_one_down, received_down[index]))
                got = jnp.where(gap >= 1, up, down)
                chunk = slot - arrivals[index]
                valid = (chunk >= 0) & (chunk < CHUNKS)
                needed = slot - due
                ready = jnp.where(needed == chunk, up, pick_chunk(held[index], needed))
                inputs.append(jnp.where((gap >= 1) & has_step, ready, 0))
                held[index] = lax.dynamic_update_index_in_dim(
                    held[index], got, jnp.where(valid, chunk, CHUNKS), 0)
                latest[index] = got
            if slot <= hop * (STEPS - 1) + CHUNKS - 1:
                total = incoming + jnp.dot(
                    jnp.concatenate(inputs, axis=1), chain_factor,
                    precision=lax.Precision.HIGH, preferred_element_type=f32)
                outgoing = jnp.where(is_solver, pick_chunk(start_value, slot - due) - total, total)

        whole = [values[:CHUNKS].reshape(padded, block)[:dates] for values in held]
        out_rows = STEPS * block // (row_count * col_count)

        def wanted(at):
            return at * col_count * out_rows // block

        source_col = row * col_count * out_rows // block // per
        stream_index = row * col_count * out_rows // block % per
        chosen = whole[0]
        for index in range(1, per):
            chosen = jnp.where(stream_index == index, whole[index], chosen)

        def piece(target):
            first = (row * col_count + target) * out_rows % block
            return lax.dynamic_slice(chosen, (jnp.int32(0), first), (dates, out_rows))

        solved = piece(col)
        for turn in range(1, col_count):
            pairs = [
                (flat(at, column(wanted(at))), flat(at, (column(wanted(at)) + turn) % col_count))
                for at in range(row_count)
            ]
            moved = send(piece((col + turn) % col_count), pairs)
            solved = jnp.where((col - source_col) % col_count == turn, moved, solved)

        away = local_order // own_points != col
        own_place = jnp.where(away, -1, local_order % own_points)
        product = lax.dot_general(
            jnp.concatenate(whole, axis=1), panel, (((1,), (1,)), ((), ())),
            precision=lax.Precision.HIGH, preferred_element_type=f32)
        left = picked(series, own_place) - product
        distance = 1
        parts = left.reshape(dates, col_count, group_rows // col_count)
        pieces = [parts[:, index] for index in range(col_count)]
        while distance < col_count:
            bit = (col // distance) % 2
            keep, give = [], []
            for index in range(0, len(pieces), 2):
                keep.append(jnp.where(bit == 0, pieces[index], pieces[index + 1]))
                give.append(jnp.where(bit == 0, pieces[index + 1], pieces[index]))
            pairs = [(flat(at, here), flat(at, here ^ distance)) for at in range(row_count) for here in range(col_count)]
            moved = send(jnp.concatenate(give, axis=1) if len(give) > 1 else give[0], pairs)
            size = group_rows // col_count
            pieces = [value + moved[:, index * size:(index + 1) * size] for index, value in enumerate(keep)]
            distance *= 2
        return solved.T, pieces[0].T

    return body


def solution(mesh):
    in_specs = (P(None, ("rows", "cols")), P("rows"), P(), P("rows", "cols"), P("rows", None))
    out_specs = (P(("rows", "cols"), None), P(("rows", "cols"), None))
    row_count, col_count = mesh.shape["rows"], mesh.shape["cols"]
    lines = row_count == STEPS and 2 * col_count == STEPS
    body = (make_line_body if lines else make_body)(row_count, col_count)
    return jax.shard_map(body, mesh=mesh, in_specs=in_specs, out_specs=out_specs, check_vma=False)
```
